32 devices in a mesh: row: 4 (over y, core), col: 8 (over z, x).
Axes of the slice: x: 2, y: 2, z: 4, core: 2. Of those that a mesh axis runs over, the one named last changes fastest.
Arguments:
- tokens: bfloat16 [52, 160, 384], P('row', 'col')
- row_sizes: int32 [4], replicated, may hold values from 1 to 13, 44 in all
- col_sizes: int32 [8], replicated, may hold values from 1 to 20, 128 in all
- norm_gain: float32 [384], replicated, may hold values from 0.25 to 1.75
- query_weight: bfloat16 [384, 384], replicated
- key_weight: bfloat16 [384, 384], replicated
- value_weight: bfloat16 [384, 384], replicated, may hold values from -0.3125 to 0.3125
- out_weight: bfloat16 [384, 384], replicated, may hold values from -0.625 to 0.625
- cache_one: bfloat16 [2, 52, 160, 384], P(None, 'row', 'col'), may hold values from -6 to 6
- gain_one: float32 [384], replicated, may hold values from 0.25 to 1.75
- conv_one: bfloat16 [3, 3, 3, 384, 384], replicated, may hold values from -0.0625 to 0.0625
- cache_two: bfloat16 [2, 104, 320, 384], P(None, 'row', 'col'), may hold values from -6 to 6
- gain_two: float32 [384], replicated, may hold values from 0.25 to 1.75
- conv_two: bfloat16 [3, 3, 3, 384, 192], replicated, may hold values from -0.0625 to 0.0625
Outputs:
- decoded: bfloat16 [104, 320, 192], P('row', 'col')
The draws below stay inside these ranges and needn't reach their ends.
Inputs may be any that keep to these rules, and one draw needn't show every extreme that they name: `row_sizes`: positive tile heights that sum to 44; the tallest has exactly 13 rows. `col_sizes`: positive tile widths that sum to 128; the widest has exactly 20 columns.
All inputs are finite; a program needn't handle non-finite values.
Results may differ from the reference program's by a relative error of at most 0.0095.
Values may be sent and summed in bfloat16 or wider, within the bound.
A program may use at most 320 MiB of HBM per device.

```python
import math
import jax
import jax.numpy as jnp
import numpy as np
from jax import lax

C = 384
C_OUT = 192
TILE_ROWS = 13
TILE_COLS = 20
LAT_ROWS = 44
LAT_COLS = 128
PAD_ROWS = 52
PAD_COLS = 160
N_ROW = 4
N_COL = 8


def draw_tokens(key, part):
    key_base, key_pix, key_chan = jax.random.split(key, 3)
    shape = (PAD_ROWS, PAD_COLS, C)
    base = jax.random.normal(key_base, shape, jnp.float32)
    pixel_scale = jnp.exp(jax.random.uniform(key_pix, (PAD_ROWS, PAD_COLS, 1), jnp.float32, -1.15, 1.15))
    chan_scale = jnp.exp(jax.random.uniform(key_chan, (C,), jnp.float32, -1.15, 1.15))
    field = base * pixel_scale * chan_scale
    return field.astype(jnp.bfloat16)


def drawn_matrix(key, factor):
    return jax.random.normal(key, (C, C), jnp.float32) * (factor / jnp.sqrt(float(C)))


def draw_query_weight(key, part):
    return drawn_matrix(jax.random.fold_in(key, 11), 4.0).astype(jnp.bfloat16)


def draw_key_weight(key, part):
    return drawn_matrix(jax.random.fold_in(key, 23), 1.0).astype(jnp.bfloat16)


def steps_of(rng, shape, cuts, low, high):
    def one(axis_at, parts):
        steps = jax.random.uniform(jax.random.fold_in(jax.random.fold_in(rng, 6), axis_at), (parts,), jnp.float32, low / len(cuts), high / len(cuts))
        return jnp.repeat(jnp.exp(steps), shape[axis_at] // parts).reshape((-1,) + (1,) * (len(shape) - axis_at - 1))

    loudness = one(*cuts[0])
    for cut in cuts[1:]:
        loudness = loudness * one(*cut)
    return loudness


def length_profile(number_of, total, reach, slope):
    portions = [(1 << 20) // math.isqrt(rank ** slope) + 1 for rank in range(2, number_of + 1)]
    spare, holding = total - reach - (number_of - 1), [1] * (number_of - 1)
    while spare > 0:
        candidates = [i for i in range(number_of - 1) if holding[i] < reach]
        pool, budget = sum([portions[i] for i in candidates]), spare
        for i in candidates:
            extra = min(reach - holding[i], max(1, budget * portions[i] // pool), spare)
            holding[i] = holding[i] + extra
            spare = spare - extra
    return np.array([reach] + holding)


def ragged(own_key, number_of, total, reach, slope):
    if number_of == 2:
        one = jax.random.randint(own_key, (), max(1, total - reach), min(reach, total - 1) + 1)
        return jnp.stack([one, total - one])
    tallies = jnp.asarray(length_profile(number_of, total, reach, slope), jnp.int32)
    pairs = (number_of - 1) // 2
    donor, sink = tallies[1:1 + 2 * pairs:2], tallies[2:2 + 2 * pairs:2]
    room = jnp.minimum(donor - 1, reach - sink)
    shifted = jax.random.randint(jax.random.fold_in(own_key, 1), (pairs,), 0, 1 << 20) % (room + 1)
    tallies = tallies.at[1:1 + 2 * pairs:2].set(donor - shifted).at[2:2 + 2 * pairs:2].set(sink + shifted)
    return tallies[jax.random.permutation(jax.random.fold_in(own_key, 2), number_of)]


def scatter_about(rng, extent, scale, most, shards=(), kind=jnp.bfloat16):
    level = steps_of(rng, extent, shards, -0.22, 0.18) if shards else 1.0
    drawn = jax.random.normal(rng, extent, jnp.float32) * scale * level
    return jnp.minimum(jnp.maximum(drawn, -most), most).astype(kind)


def setup_inputs(seed: int = 0) -> dict:
    splits = jax.random.split(jax.random.key(seed), 15)
    return {
        "tokens": draw_tokens(jax.random.fold_in(splits[14], 71), 0),
        "row_sizes": ragged(splits[1], N_ROW, LAT_ROWS, TILE_ROWS, 2).astype(jnp.int32),
        "col_sizes": ragged(splits[2], N_COL, LAT_COLS, TILE_COLS, 2).astype(jnp.int32),
        "norm_gain": jnp.clip(1.0 + 0.15 * jax.random.normal(splits[3], (C,), jnp.float32), 0.25, 1.75),
        "query_weight": draw_query_weight(jax.random.fold_in(splits[14], 71), 0),
        "key_weight": draw_key_weight(jax.random.fold_in(splits[14], 71), 0),
        "value_weight": scatter_about(splits[6], (C, C), C ** -0.5, 0.3125),
        "out_weight": scatter_about(splits[7], (C, C), (C // 4) ** -0.5, 0.625),
        "cache_one": scatter_about(splits[8], (2, PAD_ROWS, PAD_COLS, C), 1.0, 6.0, ((1, 4), (2, 8))),
        "gain_one": jnp.clip(1.0 + 0.15 * jax.random.normal(splits[9], (C,), jnp.float32), 0.25, 1.75),
        "conv_one": scatter_about(splits[10], (3, 3, 3, C, C), (27 * C) ** -0.5, 0.0625),
        "cache_two": scatter_about(splits[11], (2, 2 * PAD_ROWS, 2 * PAD_COLS, C), 1.0, 6.0, ((1, 4), (2, 8))),
        "gain_two": jnp.clip(1.0 + 0.15 * jax.random.normal(splits[12], (C,), jnp.float32), 0.25, 1.75),
        "conv_two": scatter_about(splits[13], (3, 3, 3, C, C_OUT), (27 * C) ** -0.5, 0.0625),
    }


epsilon = 1e-06

def lookup(size_table, positions):
    marks = positions[:, None] == jnp.arange(size_table.shape[0], dtype=jnp.int32)[None, :]
    return lax.optimization_barrier(jnp.sum(jnp.where(marks, size_table[None, :], 0), axis=1)).astype(jnp.int32)

def placement(extent_list, tile_len, extent_sum):
    ends = jnp.cumsum(extent_list).astype(jnp.int32)
    starts = (ends - extent_list).astype(jnp.int32)
    position = jnp.arange(extent_sum, dtype=jnp.int32)
    owner_tile = lax.optimization_barrier(jnp.sum((position[:, None] >= ends[None, :]).astype(jnp.int32), axis=1))
    first_pos = lookup(starts, owner_tile)
    return (owner_tile * tile_len + position - first_pos).astype(jnp.int32)

def spread_back(extent_list, tile_len, padded_len, extent_sum):
    ends = jnp.cumsum(extent_list).astype(jnp.int32)
    starts = (ends - extent_list).astype(jnp.int32)
    slot_index = jnp.arange(padded_len, dtype=jnp.int32)
    owner_tile = slot_index // tile_len
    local_slot = slot_index - owner_tile * tile_len
    usable = local_slot < lookup(extent_list, owner_tile)
    target = jnp.clip(lookup(starts, owner_tile) + local_slot, 0, extent_sum - 1).astype(jnp.int32)
    return (target, usable)

def rms_scale(values_in, gain_vec):
    wide = values_in.astype(jnp.float32)
    return wide * lax.rsqrt(lax.optimization_barrier(jnp.mean(wide * wide, axis=-1, keepdims=True)) + epsilon) * gain_vec

def causal_conv(frames, kernel):
    result = lax.conv_general_dilated(frames[None].astype(jnp.float32), kernel.astype(jnp.float32), (1, 1, 1), ((0, 0), (1, 1), (1, 1)), dimension_numbers=('NDHWC', 'DHWIO', 'NDHWC'), precision=lax.Precision.HIGHEST)
    return result[0, 0]

def reference(tokens, row_sizes, col_sizes, norm_gain, query_weight, key_weight, value_weight, out_weight, cache_one, gain_one, conv_one, cache_two, gain_two, conv_two):
    channels = tokens.shape[-1]
    row_map = placement(row_sizes, TILE_ROWS, LAT_ROWS)
    col_map = placement(col_sizes, TILE_COLS, LAT_COLS)
    row_fine = placement(2 * row_sizes, 2 * TILE_ROWS, 2 * LAT_ROWS)
    col_fine = placement(2 * col_sizes, 2 * TILE_COLS, 2 * LAT_COLS)
    frame = jnp.take(jnp.take(tokens, row_map, axis=0), col_map, axis=1)
    prior_one = jnp.take(jnp.take(cache_one, row_map, axis=1), col_map, axis=2)
    prior_two = jnp.take(jnp.take(cache_two, row_fine, axis=1), col_fine, axis=2)
    count = LAT_ROWS * LAT_COLS
    normed = rms_scale(frame, norm_gain).astype(jnp.bfloat16).reshape(count, channels)
    queries = jnp.dot(normed, query_weight, preferred_element_type=jnp.float32).astype(jnp.bfloat16)
    key_rows = jnp.dot(normed, key_weight, preferred_element_type=jnp.float32).astype(jnp.bfloat16)
    value_rows = jnp.dot(normed, value_weight, preferred_element_type=jnp.float32).astype(jnp.bfloat16)
    scale = 1.0 / math.sqrt(channels)
    block = math.gcd(count, 1024)

    def one_block(query_block):
        scores = jnp.dot(query_block, key_rows.T, preferred_element_type=jnp.float32) * scale
        highest = lax.optimization_barrier(jnp.max(scores, axis=1, keepdims=True))
        expos = jnp.exp(scores - highest)
        denominator = lax.optimization_barrier(jnp.sum(expos, axis=1, keepdims=True))
        probs = expos.astype(jnp.bfloat16)
        return (jnp.dot(probs, value_rows, preferred_element_type=jnp.float32) / denominator).astype(jnp.bfloat16)
    attention = lax.map(one_block, queries.reshape(count // block, block, channels)).reshape(count, channels)
    projected = jnp.dot(attention, out_weight, preferred_element_type=jnp.float32)
    mixed = (frame.astype(jnp.float32) + projected.reshape(LAT_ROWS, LAT_COLS, channels)).astype(jnp.bfloat16)
    act_one = jax.nn.silu(rms_scale(mixed, gain_one)).astype(jnp.bfloat16)
    frames_one = jnp.concatenate([prior_one, act_one[None]], axis=0)
    y_one = causal_conv(frames_one, conv_one).astype(jnp.bfloat16)
    act_small = jax.nn.silu(rms_scale(y_one, gain_two)).astype(jnp.bfloat16)
    act_two = jnp.repeat(jnp.repeat(act_small, 2, axis=0), 2, axis=1)
    frames_two = jnp.concatenate([prior_two, act_two[None]], axis=0)
    y_two = causal_conv(frames_two, conv_two).astype(jnp.bfloat16)
    row_target, row_usable = spread_back(2 * row_sizes, 2 * TILE_ROWS, 2 * PAD_ROWS, 2 * LAT_ROWS)
    col_target, col_usable = spread_back(2 * col_sizes, 2 * TILE_COLS, 2 * PAD_COLS, 2 * LAT_COLS)
    placed = jnp.take(jnp.take(y_two, row_target, axis=0), col_target, axis=1)
    usable = (row_usable[:, None] & col_usable[None, :])[:, :, None]
    return jnp.where(usable, placed, jnp.zeros_like(placed)).astype(jnp.bfloat16)
```

```python
import functools
import math

import jax
import jax.numpy as jnp
from jax import lax
from jax.experimental import pallas as pl
from jax.experimental.pallas import tpu as pltpu
from jax.sharding import PartitionSpec as P

epsilon = 1e-06
masked_score = -1e30
f32 = jnp.float32
bf16 = jnp.bfloat16
MESH = pl.DeviceIdType.MESH
steps = ((-1, 0), (1, 0), (0, -1), (0, 1), (-1, -1), (-1, 1), (1, -1), (1, 1))
vmem_bytes = 58 * 1024 * 1024


def round_up(value, unit):
    return -(-value // unit) * unit


def select_size(size_table, position):
    marks = jnp.arange(size_table.shape[0], dtype=jnp.int32) == position
    return jnp.sum(jnp.where(marks, size_table, 0))


def rms_scale(wide, gain_vec):
    return wide * lax.rsqrt(jnp.mean(wide * wide, axis=-1, keepdims=True) + epsilon) * gain_vec


def silu(wide):
    return wide / (1.0 + jnp.exp(-wide))


def times(left, right):
    return jnp.dot(left, right, preferred_element_type=f32)


def times_t(left, right):
    return lax.dot_general(left, right, (((1,), (1,)), ((), ())), preferred_element_type=f32)


def wrapped(position, step, count):
    return lax.rem(position + step + count, count)


def partner(counts, step):
    return (
        wrapped(lax.axis_index("row"), step[0], counts[0]),
        wrapped(lax.axis_index("col"), step[1], counts[1]),
    )


def greet(devices):
    barrier = pltpu.get_barrier_semaphore()
    for device in devices:
        pl.semaphore_signal(barrier, inc=1, device_id=device, device_id_type=MESH)
    pl.semaphore_wait(barrier, len(devices))


def iota3(shape, dim):
    return lax.broadcasted_iota(jnp.int32, shape, dim)


def halo_copies(counts, sent, got, send_sems, recv_sems):
    return [
        pltpu.make_async_remote_copy(
            src_ref=sent.at[k],
            dst_ref=got.at[k],
            send_sem=send_sems.at[k],
            recv_sem=recv_sems.at[k],
            device_id=partner(counts, step),
            device_id_type=MESH,
        )
        for k, step in enumerate(steps)
    ]


def put_pieces(frame, f, tall, wide, sent):
    height, breadth, channels = frame.shape
    rows = iota3(frame.shape, 0)
    cols = iota3(frame.shape, 1)
    left = jnp.sum(jnp.where(cols == 0, frame, 0.0), axis=1)
    right = jnp.sum(jnp.where(cols == wide - 1, frame, 0.0), axis=1)
    side_rows = iota3(left.shape, 0)
    sent[0, f, 0:breadth, :] = frame[0].astype(bf16)
    sent[1, f, 0:breadth, :] = jnp.sum(jnp.where(rows == tall - 1, frame, 0.0), axis=0).astype(bf16)
    sent[2, f, 0:height, :] = left.astype(bf16)
    sent[3, f, 0:height, :] = right.astype(bf16)
    for k, side in ((4, left), (5, right)):
        sent[k, f, 0:16, :] = jnp.broadcast_to(side[0:1], (16, channels)).astype(bf16)
        low = jnp.sum(jnp.where(side_rows == tall - 1, side, 0.0), axis=0, keepdims=True)
        sent[k + 2, f, 0:16, :] = jnp.broadcast_to(low, (16, channels)).astype(bf16)


def extend(frame, f, tall, wide, got, counts, shifted):
    height, breadth, channels = frame.shape
    row, col = lax.axis_index("row"), lax.axis_index("col")

    def piece(k):
        ok = None
        step = steps[k]
        if step[0] != 0:
            ok = (row > 0) if step[0] > 0 else (row < counts[0] - 1)
        if step[1] != 0:
            ok_col = (col > 0) if step[1] > 0 else (col < counts[1] - 1)
            ok = ok_col if ok is None else jnp.logical_and(ok, ok_col)
        return got[k, f].astype(f32) * jnp.where(ok, 1.0, 0.0)

    below, above = piece(0)[0:breadth], piece(1)[0:breadth]
    right_side, left_side = piece(2), piece(3)
    right_low, left_low = piece(4)[0:1], piece(5)[0:1]
    right_top, left_top = piece(6)[0:1], piece(7)[0:1]
    line_cols = iota3((breadth, channels), 0)
    below = jnp.where(line_cols == wide, right_low, below)
    above = jnp.where(line_cols == wide, right_top, above)
    size = (height + 2) * breadth
    for r in range(height + 2):
        if r == 0:
            line, first = above, left_top
        else:
            if r <= height:
                line = jnp.where(line_cols == wide, right_side[r - 1 : r], frame[r - 1])
                first = left_side[r - 1 : r]
                line = jnp.where(tall + 1 == r, below, line)
                first = jnp.where(tall + 1 == r, left_low, first)
            else:
                line, first = below, left_low
        before = jnp.where(line_cols == 0, first, pltpu.roll(line, 1, 0))
        after = pltpu.roll(line, breadth - 1, 0)
        place = slice(r * breadth, (r + 1) * breadth)
        shifted[f, 0, place, :] = before.astype(bf16)
        shifted[f, 1, place, :] = line.astype(bf16)
        shifted[f, 2, place, :] = after.astype(bf16)


def chunk_of(total):
    for size in (208, 128, 64, 32, 16):
        if total % size == 0:
            return size
    return total


def prior_kernel(
    counts, sizes, cache_one, cache_two, conv_one, conv_two, sum_one, sum_two,
    sent_one, got_one, sent_two, got_two, shifted_one, shifted_two, send_sems, recv_sems,
):
    tall, wide = sizes[0], sizes[1]
    greet([partner(counts, step) for step in steps])
    work = (
        (cache_one, conv_one, sum_one, sent_one, got_one, shifted_one, 1, times),
        (cache_two, conv_two, sum_two, sent_two, got_two, shifted_two, 2, times_t),
    )
    sets = []
    for i, (cache, _, _, sent, got, _, fine, _) in enumerate(work):
        for f in range(2):
            put_pieces(cache[f].astype(f32), f, fine * tall, fine * wide, sent)
        copies = halo_copies(counts, sent, got, send_sems.at[i], recv_sems.at[i])
        for copy in copies:
            copy.start()
        sets.append(copies)
    for copies, (cache, conv, total, sent, got, shifted, fine, product) in zip(sets, work):
        for copy in copies:
            copy.wait()
        for f in range(2):
            extend(cache[f].astype(f32), f, fine * tall, fine * wide, got, counts, shifted)
        breadth = cache.shape[2]
        size = chunk_of(total.shape[0])

        @pl.loop(0, total.shape[0] // size)
        def _(step):
            start = pl.multiple_of(step * size, 16)
            part = jnp.zeros((size, total.shape[1]), f32)
            for f in range(2):
                for a in range(3):
                    for b in range(3):
                        rows = shifted[f, b, pl.ds(start + a * breadth, size), :]
                        part += product(rows, conv[f * 9 + a * 3 + b])
            total[pl.ds(start, size), :] = part


def score_kernel(queries, keys, bias, out):
    scores = times_t(queries[0], keys[...]) + bias[...]
    highest = jnp.max(scores, axis=1, keepdims=True)
    expos = jnp.exp(scores - highest)
    total = jnp.sum(expos, axis=1, keepdims=True)
    mean = times(expos.astype(bf16), keys[...]) / total
    channels = mean.shape[1]
    level = highest + jnp.log(total)
    high = level.astype(bf16).astype(f32)
    mid = (level - high).astype(bf16).astype(f32)
    low = level - high - mid
    lanes = lax.broadcasted_iota(jnp.int32, (mean.shape[0], 128), 1)
    coded = jnp.where(lanes == 0, high, jnp.where(lanes == 1, mid, jnp.where(lanes == 2, low, 0.0)))
    out[0, :, 0:channels] = mean.astype(bf16)
    out[0, :, channels : channels + 128] = coded.astype(bf16)


def tail_kernel(
    counts, sizes, parts, tokens, value_weight, out_weight, gain_one, gain_two,
    sum_one, sum_two, conv_one, conv_two, out,
    got_parts, sent_one, got_one, sent_two, got_two, shifted_one, shifted_two, small, fine_sum,
    part_send, part_recv, send_sems, recv_sems,
):
    row_count = counts[0]
    tall, wide = sizes[0], sizes[1]
    row, col = lax.axis_index("row"), lax.axis_index("col")
    others = [(wrapped(row, d, row_count), col) for d in range(1, row_count)]
    greet(others + [partner(counts, step) for step in steps if step[1] != 0])
    copies = []
    for d, device in enumerate(others):
        copies.append(
            pltpu.make_async_remote_copy(
                src_ref=parts.at[device[0]],
                dst_ref=got_parts.at[d],
                send_sem=part_send.at[d],
                recv_sem=part_recv.at[d],
                device_id=device,
                device_id_type=MESH,
            )
        )
        copies[-1].start()
    for copy in copies:
        copy.wait()
    height, narrow, channels = tokens.shape
    blocks = [parts[row]] + [got_parts[d] for d in range(row_count - 1)]
    levels = [
        jnp.sum(block[:, channels : channels + 128].astype(f32), axis=1, keepdims=True)
        for block in blocks
    ]
    top = functools.reduce(jnp.maximum, levels)
    weights = [jnp.exp(level - top) for level in levels]
    total = functools.reduce(jnp.add, weights)
    mean = functools.reduce(
        jnp.add, [w * block[:, 0:channels].astype(f32) for w, block in zip(weights, blocks)]
    )
    mean = (mean / total).astype(bf16)
    attention = times(mean, value_weight[...]).astype(bf16)
    projected = times(attention, out_weight[...])
    mixed = tokens[...].astype(f32).reshape(height * narrow, channels) + projected
    mixed = mixed.astype(bf16).astype(f32)
    act_one = silu(rms_scale(mixed, gain_one[...])).reshape(height, narrow, channels)
    breadth = small.shape[1]
    small[:, 0:narrow, :] = act_one
    small[:, narrow:breadth, :] = jnp.zeros((height, breadth - narrow, channels), f32)
    frame = small[...]
    put_pieces(frame, 0, tall, wide, sent_one)
    halos = halo_copies(counts, sent_one, got_one, send_sems.at[0], recv_sems.at[0])
    for copy in halos:
        copy.start()
    for copy in halos:
        copy.wait()
    extend(frame, 0, tall, wide, got_one, counts, shifted_one)
    size = height * breadth
    y_one = sum_one[...]
    for a in range(3):
        for b in range(3):
            y_one += times(shifted_one[0, b, a * breadth : a * breadth + size, :], conv_one[a * 3 + b])
    y_one = y_one.astype(bf16).astype(f32)
    frame = silu(rms_scale(y_one, gain_two[...])).reshape(height, breadth, channels)
    put_pieces(frame, 0, tall, wide, sent_two)
    halos = halo_copies(counts, sent_two, got_two, send_sems.at[1], recv_sems.at[1])
    for copy in halos:
        copy.start()
    for copy in halos:
        copy.wait()
    extend(frame, 0, tall, wide, got_two, counts, shifted_two)
    for p in range(2):
        for q in range(2):
            phase = jnp.zeros((size, conv_two.shape[1]), f32)
            for a in range(2):
                for b in range(2):
                    first = (p + a) * breadth
                    phase += times_t(
                        shifted_two[0, q + b, first : first + size, :],
                        conv_two[p * 8 + q * 4 + a * 2 + b],
                    )
            for i in range(height):
                for lane in range(fine_sum.shape[0]):
                    fine_sum[lane, 2 * i + p, pl.ds(q, breadth, stride=2), :] = phase[
                        i * breadth : (i + 1) * breadth, lane * 128 : (lane + 1) * 128
                    ]
    fine_height, fine_narrow, channels_out = out.shape
    fine_breadth = sum_two.shape[1]
    fine_cols = lax.broadcasted_iota(jnp.int32, (fine_narrow, channels_out), 0)
    for i in range(fine_height):
        keep = jnp.logical_and(fine_cols < 2 * wide, i < 2 * tall)
        for lane in range(fine_sum.shape[0]):
            place = slice(lane * 128, min(lane * 128 + 128, channels_out))
            count = place.stop - place.start
            line = fine_sum[lane, i, 0:fine_narrow, 0:count] + sum_two[i, 0:fine_narrow, place]
            out[i, :, place] = jnp.where(keep[:, place], line, 0.0).astype(bf16)


def remote_call(kernel, out_shape, kinds, scratch, number, flops):
    return pl.pallas_call(
        kernel,
        out_shape=out_shape,
        in_specs=[pl.BlockSpec(memory_space=kind) for kind in kinds],
        out_specs=jax.tree.map(lambda _: pl.BlockSpec(memory_space=pltpu.VMEM), out_shape),
        scratch_shapes=scratch,
        compiler_params=pltpu.CompilerParams(
            collective_id=number, has_side_effects=True, vmem_limit_bytes=vmem_bytes
        ),
        cost_estimate=pl.CostEstimate(flops=flops, bytes_accessed=20_000_000, transcendentals=0),
    )


def local(
    counts, tokens, row_sizes, col_sizes, norm_gain, query_weight, key_weight, value_weight,
    out_weight, cache_one, gain_one, conv_one, cache_two, gain_two, conv_two,
):
    height, width, channels = tokens.shape
    channels_out = conv_two.shape[-1]
    rows, cols = counts
    narrow = round_up(width, 8)
    breadth = round_up(width + 1, 16)
    fine_breadth = round_up(2 * width + 1, 16)
    each = height * narrow
    row_count = select_size(row_sizes, lax.axis_index("row"))
    col_count = select_size(col_sizes, lax.axis_index("col"))
    sizes = jnp.stack([row_count, col_count]).astype(jnp.int32)

    padded = jnp.pad(tokens, ((0, 0), (0, narrow - width), (0, 0)))
    normed = rms_scale(padded.astype(f32), norm_gain).astype(bf16).reshape(each, channels)
    queries = times(normed, query_weight).astype(bf16)
    queries = (times_t(queries, key_weight) * (1.0 / math.sqrt(channels))).astype(bf16)
    all_keys = lax.all_gather(normed, "col", axis=0, tiled=True)
    all_queries = lax.all_gather(queries, "row", axis=0)

    wide_one = jnp.pad(cache_one, ((0, 0), (0, 0), (0, breadth - width), (0, 0)))
    wide_two = jnp.pad(cache_two, ((0, 0), (0, 0), (0, fine_breadth - 2 * width), (0, 0)))
    flipped = jnp.swapaxes(conv_two, 3, 4)
    line_one = max(breadth, round_up(height, 16))
    line_two = max(fine_breadth, round_up(2 * height, 16))
    vm = pltpu.VMEM
    sum_one, sum_two = remote_call(
        functools.partial(prior_kernel, counts),
        (
            jax.ShapeDtypeStruct((height * breadth, channels), f32),
            jax.ShapeDtypeStruct((2 * height * fine_breadth, channels_out), f32),
        ),
        [pltpu.SMEM] + [vm] * 4,
        [
            vm((8, 2, line_one, channels), bf16),
            vm((8, 2, line_one, channels), bf16),
            vm((8, 2, line_two, channels), bf16),
            vm((8, 2, line_two, channels), bf16),
            vm((2, 3, (height + 2) * breadth, channels), bf16),
            vm((2, 3, (2 * height + 2) * fine_breadth, channels), bf16),
            pltpu.SemaphoreType.DMA((2, 8)),
            pltpu.SemaphoreType.DMA((2, 8)),
        ],
        1,
        9_000_000_000,
    )(
        sizes,
        wide_one,
        wide_two,
        conv_one[:2].reshape(18, channels, channels),
        flipped[:2].reshape(18, channels_out, channels),
    )
    sum_two = sum_two.reshape(2 * height, fine_breadth, channels_out)

    last = flipped[2].astype(f32)
    by_row = [[last[0], last[1] + last[2]], [last[0] + last[1], last[2]]]
    phases = []
    for p in range(2):
        for q in range(2):
            for a in range(2):
                line = by_row[p][a]
                pair = [line[0], line[1] + line[2]] if q == 0 else [line[0] + line[1], line[2]]
                phases.extend(pair)
    phase_weights = jnp.stack(phases).astype(bf16)
    phase_weights = jnp.pad(phase_weights, ((0, 0), (0, round_up(channels_out, 128) - channels_out), (0, 0)))

    slot_row = lax.broadcasted_iota(jnp.int32, (height, narrow), 0)
    slot_col = lax.broadcasted_iota(jnp.int32, (height, narrow), 1)
    usable = (slot_row < row_count)[None] & (slot_col[None] < col_sizes[:, None, None])
    bias = jnp.where(usable, 0.0, masked_score).astype(f32).reshape(1, cols * each)
    parts = pl.pallas_call(
        score_kernel,
        grid=(rows,),
        out_shape=jax.ShapeDtypeStruct((rows, each, channels + 128), bf16),
        in_specs=[
            pl.BlockSpec((1, each, channels), lambda i: (i, 0, 0)),
            pl.BlockSpec((cols * each, channels), lambda i: (0, 0)),
            pl.BlockSpec((1, cols * each), lambda i: (0, 0)),
        ],
        out_specs=pl.BlockSpec((1, each, channels + 128), lambda i: (i, 0, 0)),
        compiler_params=pltpu.CompilerParams(vmem_limit_bytes=vmem_bytes),
    )(all_queries, all_keys, bias)

    return remote_call(
        functools.partial(tail_kernel, counts),
        jax.ShapeDtypeStruct((2 * height, 2 * width, channels_out), bf16),
        [pltpu.SMEM] + [vm] * 10,
        [
            vm((rows - 1, each, channels + 128), bf16),
            vm((8, 1, line_one, channels), bf16),
            vm((8, 1, line_one, channels), bf16),
            vm((8, 1, line_one, channels), bf16),
            vm((8, 1, line_one, channels), bf16),
            vm((1, 3, (height + 2) * breadth, channels), bf16),
            vm((1, 3, (height + 2) * breadth, channels), bf16),
            vm((height, breadth, channels), f32),
            vm((round_up(channels_out, 128) // 128, 2 * height, 2 * breadth, 128), f32),
            pltpu.SemaphoreType.DMA((rows - 1,)),
            pltpu.SemaphoreType.DMA((rows - 1,)),
            pltpu.SemaphoreType.DMA((2, 8)),
            pltpu.SemaphoreType.DMA((2, 8)),
        ],
        2,
        3_000_000_000,
    )(
        sizes,
        parts,
        padded,
        value_weight,
        out_weight,
        gain_one.reshape(1, channels),
        gain_two.reshape(1, channels),
        sum_one,
        sum_two,
        conv_one[2].reshape(9, channels, channels),
        phase_weights,
    )


def solution(mesh):
    tiled = P("row", "col", None)
    framed = P(None, "row", "col", None)
    placed = (tiled,) + (P(),) * 7 + (framed, P(), P(), framed, P(), P())
    counts = (mesh.shape["row"], mesh.shape["col"])
    return jax.shard_map(
        functools.partial(local, counts),
        mesh=mesh,
        in_specs=placed,
        out_specs=P("row", "col", None),
        check_vma=False,
    )
```

```python
import functools
import math

import jax
import jax.numpy as jnp
from jax import lax
from jax.experimental import pallas as pl
from jax.experimental.pallas import tpu as pltpu
from jax.sharding import PartitionSpec as P

epsilon = 1e-06
masked_score = -1e30
f32 = jnp.float32
bf16 = jnp.bfloat16
MESH = pl.DeviceIdType.MESH
steps = ((-1, 0), (1, 0), (0, -1), (0, 1), (-1, -1), (-1, 1), (1, -1), (1, 1))
vmem_bytes = 58 * 1024 * 1024


def round_up(value, unit):
    return -(-value // unit) * unit


def rms_scale(wide, gain_vec):
    return wide * lax.rsqrt(jnp.mean(wide * wide, axis=-1, keepdims=True) + epsilon) * gain_vec


def silu(wide):
    return wide / (1.0 + jnp.exp(-wide))


def times(left, right):
    return jnp.dot(left, right, preferred_element_type=f32)


def times_t(left, right):
    return lax.dot_general(left, right, (((1,), (1,)), ((), ())), preferred_element_type=f32)


def wrapped(position, step, count):
    return lax.rem(position + step + count, count)


def partner(counts, step):
    return (
        wrapped(lax.axis_index("row"), step[0], counts[0]),
        wrapped(lax.axis_index("col"), step[1], counts[1]),
    )


def greet(devices):
    barrier = pltpu.get_barrier_semaphore()
    for device in devices:
        pl.semaphore_signal(barrier, inc=1, device_id=device, device_id_type=MESH)
    pl.semaphore_wait(barrier, len(devices))


def iota3(shape, dim):
    return lax.broadcasted_iota(jnp.int32, shape, dim)


def halo_copies(counts, sent, got, send_sems, recv_sems):
    return [
        pltpu.make_async_remote_copy(
            src_ref=sent.at[k],
            dst_ref=got.at[k],
            send_sem=send_sems.at[k],
            recv_sem=recv_sems.at[k],
            device_id=partner(counts, step),
            device_id_type=MESH,
        )
        for k, step in enumerate(steps)
    ]


def put_pieces(frame, last_line, f, tall, wide, sent):
    height, breadth, channels = frame.shape
    cols = iota3(frame.shape, 1)
    left = jnp.concatenate([frame[r, 0:1, :] for r in range(height)], axis=0)
    right = jnp.sum(jnp.where(cols == wide - 1, frame, 0.0), axis=1)
    side_rows = iota3(left.shape, 0)
    sent[0, f, 0:breadth, :] = frame[0].astype(bf16)
    sent[1, f, 0:breadth, :] = last_line.astype(bf16)
    sent[2, f, 0:height, :] = left.astype(bf16)
    sent[3, f, 0:height, :] = right.astype(bf16)
    for k, side in ((4, left), (5, right)):
        sent[k, f, 0:16, :] = jnp.broadcast_to(side[0:1], (16, channels)).astype(bf16)
        low = jnp.sum(jnp.where(side_rows == tall - 1, side, 0.0), axis=0, keepdims=True)
        sent[k + 2, f, 0:16, :] = jnp.broadcast_to(low, (16, channels)).astype(bf16)


def extend(frame, f, tall, wide, got, counts, shifted):
    height, breadth, channels = frame.shape
    row, col = lax.axis_index("row"), lax.axis_index("col")

    def piece(k):
        ok = None
        step = steps[k]
        if step[0] != 0:
            ok = (row > 0) if step[0] > 0 else (row < counts[0] - 1)
        if step[1] != 0:
            ok_col = (col > 0) if step[1] > 0 else (col < counts[1] - 1)
            ok = ok_col if ok is None else jnp.logical_and(ok, ok_col)
        return got[k, f].astype(f32) * jnp.where(ok, 1.0, 0.0)

    below, above = piece(0)[0:breadth], piece(1)[0:breadth]
    right_side, left_side = piece(2), piece(3)
    right_low, left_low = piece(4)[0:1], piece(5)[0:1]
    right_top, left_top = piece(6)[0:1], piece(7)[0:1]
    line_cols = iota3((breadth, channels), 0)
    below = jnp.where(line_cols == wide, right_low, below)
    above = jnp.where(line_cols == wide, right_top, above)
    size = (height + 2) * breadth
    for r in range(height + 2):
        if r == 0:
            line, first = above, left_top
        else:
            if r <= height:
                line = jnp.where(line_cols == wide, right_side[r - 1 : r], frame[r - 1])
                first = left_side[r - 1 : r]
                line = jnp.where(tall + 1 == r, below, line)
                first = jnp.where(tall + 1 == r, left_low, first)
            else:
                line, first = below, left_low
        before = jnp.where(line_cols == 0, first, pltpu.roll(line, 1, 0))
        after = pltpu.roll(line, breadth - 1, 0)
        place = slice(r * breadth, (r + 1) * breadth)
        shifted[f, 0, place, :] = before.astype(bf16)
        shifted[f, 1, place, :] = line.astype(bf16)
        shifted[f, 2, place, :] = after.astype(bf16)


def widened(frame, breadth):
    frame = frame.astype(f32)
    gap = breadth - frame.shape[-2]
    if gap == 0:
        return frame
    zeros = jnp.zeros(frame.shape[:-2] + (gap, frame.shape[-1]), f32)
    return jnp.concatenate([frame, zeros], axis=-2)


def key_spread(counts, keys, sems):
    fwd_sems, bwd_sems, fast_sems, recv_sems = sems
    cols = counts[1]
    fast = fast_part(cols)
    slow = cols // fast
    row, col = lax.axis_index("row"), lax.axis_index("col")
    s, f = col // fast, col % fast

    def copy_to(block, sem, slow_at, fast_at):
        return pltpu.make_async_remote_copy(
            src_ref=keys.at[block],
            dst_ref=keys.at[block],
            send_sem=sem,
            recv_sem=recv_sems.at[block],
            device_id=(row, slow_at * fast + fast_at),
            device_id_type=MESH,
        )

    def fast_copies(block_s):
        return [
            copy_to(block_s * fast + f, fast_sems.at[d - 1, block_s], s, (f + d) % fast)
            for d in range(1, fast)
        ]

    def line_copy(hop, up):
        block_s = s - hop if up else s + hop
        sems_at = fwd_sems if up else bwd_sems
        return copy_to(block_s * fast + f, sems_at.at[hop], s + 1 if up else s - 1, f)

    def goes(hop, up):
        if up:
            return jnp.logical_and(s - hop >= 0, s + 1 < slow)
        return jnp.logical_and(s + hop < slow, s - 1 >= 0)

    def start():
        for up in (True, False):
            @pl.when(goes(0, up))
            def _():
                line_copy(0, up).start()

        for copy in fast_copies(s):
            copy.start()

    def hop(step):
        for up in (True, False):
            came = (s - step >= 0) if up else (s + step < slow)

            @pl.when(came)
            def _():
                block_s = s - step if up else s + step
                copy_to(block_s * fast + f, fwd_sems.at[0], s, f).wait_recv()
                for copy in fast_copies(block_s):
                    copy.start()

            if step < slow - 1:
                @pl.when(goes(step, up))
                def _():
                    line_copy(step, up).start()

    def finish():
        for block_s in range(slow):
            for d in range(1, fast):
                copy_to(block_s * fast + (f + d) % fast, fwd_sems.at[0], s, f).wait_recv()
            for copy in fast_copies(block_s):
                copy.wait_send()
        for step in range(slow - 1):
            for up in (True, False):
                @pl.when(goes(step, up))
                def _():
                    line_copy(step, up).wait_send()

    greeted = [(row, s * fast + (f + d) % fast) for d in range(1, fast)]
    return start, hop, finish, greeted, slow


def fast_part(cols):
    fast = 1 << ((cols.bit_length() - 1) // 2)
    return fast if cols % fast == 0 else 1


def convolve_rows(shifted, frames, conv, product, start, size, breadth):
    part = None
    for f in range(frames):
        for a in range(3):
            for b in range(3):
                rows = shifted[f, b, start + a * breadth : start + a * breadth + size, :]
                term = product(rows, conv[f * 9 + a * 3 + b])
                part = term if part is None else part + term
    return part


def prior_kernel(
    counts, row_sizes, col_sizes, tokens, norm_gain, query_weight, key_weight,
    cache_one, cache_two, conv_one, conv_two,
    sum_one, sum_two, keys, queries, phase_weights,
    sent_one, got_one, sent_two, got_two, shifted_one, shifted_two, held_one, held_two,
    send_sems, recv_sems, query_send, query_recv, fwd_sems, bwd_sems, fast_sems, key_recv, load_sems,
):
    row_count, col_count = counts
    row, col = lax.axis_index("row"), lax.axis_index("col")
    tall, wide = row_sizes[row], col_sizes[col]
    loads = [
        pltpu.make_async_copy(conv_two, held_two, load_sems.at[0]),
        pltpu.make_async_copy(conv_one.at[0:18], held_one, load_sems.at[1]),
    ]
    for load in loads:
        load.start()
    key_sems = (fwd_sems, bwd_sems, fast_sems, key_recv)
    start, hop, finish, fast_others, slow = key_spread(counts, keys, key_sems)
    fast = col_count // slow
    line = [
        (row, wrapped(col, step * fast, col_count)) for step in ((1, -1) if slow > 1 else ())
    ]
    others = [(wrapped(row, d, row_count), col) for d in range(1, row_count)]
    greet(
        others + fast_others + line
        + [partner(counts, step) for step in steps if step[1] != 0]
    )
    normed = rms_scale(tokens[...].astype(f32), norm_gain[...][None, :]).astype(bf16)
    keys[col] = normed
    start()
    query = times(normed, query_weight[...]).astype(bf16)
    unit = math.log2(math.e) / math.sqrt(tokens.shape[1])
    queries[row] = (times_t(query, key_weight[...]) * unit).astype(bf16)
    query_copies = [
        pltpu.make_async_remote_copy(
            src_ref=queries.at[row],
            dst_ref=queries.at[row],
            send_sem=query_send.at[d],
            recv_sem=query_recv.at[d],
            device_id=device,
            device_id_type=MESH,
        )
        for d, device in enumerate(others)
    ]
    for copy in query_copies:
        copy.start()
    breadth, fine_breadth = cache_one.shape[2], round_up(cache_two.shape[2] + 1, 16)
    for f in range(2):
        last_line = cache_one[f, jnp.maximum(tall, 1) - 1].astype(f32)
        put_pieces(cache_one[f].astype(f32), last_line, f, tall, wide, sent_one)
    halos_one = halo_copies(counts, sent_one, got_one, send_sems.at[0], recv_sems.at[0])
    for copy in halos_one:
        copy.start()
    for f in range(2):
        last_line = widened(cache_two[f, 2 * jnp.maximum(tall, 1) - 1], fine_breadth)
        frame = widened(cache_two[f], fine_breadth)
        put_pieces(frame, last_line, f, 2 * tall, 2 * wide, sent_two)
    halos_two = halo_copies(counts, sent_two, got_two, send_sems.at[1], recv_sems.at[1])
    for copy in halos_two:
        copy.start()
    if slow > 1:
        hop(1)
    loads[0].wait()
    channels_out = held_two.shape[1]
    phase_weights[:, channels_out:, :] = jnp.zeros_like(phase_weights[:, channels_out:, :])
    for p in range(2):
        for q in range(2):
            for a in range(2):
                for b in range(2):
                    rows_in = ((0,), (1, 2))[a] if p == 0 else ((0, 1), (2,))[a]
                    cols_in = ((0,), (1, 2))[b] if q == 0 else ((0, 1), (2,))[b]
                    taps = [held_two[18 + 3 * i + j].astype(f32) for i in rows_in for j in cols_in]
                    total = functools.reduce(jnp.add, taps).astype(bf16)
                    phase_weights[p * 8 + q * 4 + a * 2 + b, 0:channels_out, :] = total
    for copy in halos_one:
        copy.wait()
    for f in range(2):
        extend(cache_one[f].astype(f32), f, tall, wide, got_one, counts, shifted_one)
    if slow > 2:
        hop(2)
    loads[1].wait()
    sum_one[...] = convolve_rows(
        shifted_one, 2, held_one, times, 0, sum_one.shape[0], breadth
    )
    for step in range(3, slow):
        hop(step)
    for copy in halos_two:
        copy.wait()
    for f in range(2):
        frame = widened(cache_two[f], fine_breadth)
        extend(frame, f, 2 * tall, 2 * wide, got_two, counts, shifted_two)
    total = sum_two.shape[0]
    size = total // 3 if total % 48 == 0 else total
    for at in range(0, total, size):
        sum_two[at : at + size, :] = convolve_rows(
            shifted_two, 2, held_two, times_t, at, size, fine_breadth
        )
    finish()
    for copy in query_copies:
        copy.wait()


def tail_kernel(
    counts, width, row_sizes, col_sizes, queries, keys, tokens, value_weight, out_weight,
    gain_one, gain_two, sum_one, sum_two, conv_two, conv_one, out,
    parts, bias, held_one, got_parts, sent_one, got_one, sent_two, got_two,
    shifted_one, shifted_two, flat, small, fine_sum,
    part_send, part_recv, send_sems, recv_sems, load_sem,
):
    row_count, col_count = counts
    row, col = lax.axis_index("row"), lax.axis_index("col")
    tall, wide = row_sizes[row], col_sizes[col]
    load = pltpu.make_async_copy(conv_one.at[18:27], held_one, load_sem)
    load.start()
    others = [(wrapped(row, d, row_count), col) for d in range(1, row_count)]
    greet(others + [partner(counts, step) for step in steps if step[1] != 0])
    each, channels = tokens.shape
    height, breadth, _ = small.shape
    slot = lax.broadcasted_iota(jnp.int32, (1, each), 1)
    slot_row = jnp.zeros((1, each), jnp.int32)
    for r in range(1, height + 1):
        slot_row += jnp.where(slot >= r * width, 1, 0)
    slot_col = slot - slot_row * width
    for c in range(col_count):
        usable = jnp.logical_and(slot_row < tall, slot_col < col_sizes[c])
        bias[c : c + 1, :] = jnp.where(usable, 0.0, masked_score)
    masks = jnp.concatenate([bias[c : c + 1, :] for c in range(col_count)], axis=1)
    lanes = lax.broadcasted_iota(jnp.int32, (each, 128), 1)

    def partial_of(target):
        all_keys = keys[...].reshape(col_count * each, channels)
        scores = times_t(queries[target], all_keys) + masks
        highest = jnp.max(scores, axis=1, keepdims=True)
        expos = jnp.exp2(scores - highest)
        total = jnp.sum(expos, axis=1, keepdims=True)
        mean = times(expos.astype(bf16), all_keys) / total
        level = highest + jnp.log2(total)
        high = level.astype(bf16).astype(f32)
        mid = (level - high).astype(bf16).astype(f32)
        low = level - high - mid
        coded = jnp.where(lanes == 0, high, jnp.where(lanes == 1, mid, jnp.where(lanes == 2, low, 0.0)))
        parts[target, :, 0:channels] = mean.astype(bf16)
        parts[target, :, channels : channels + 128] = coded.astype(bf16)

    copies = []
    for d in sorted(range(1, row_count), key=lambda d: -min(d, row_count - d)):
        target = others[d - 1][0]
        partial_of(target)
        copies.append(
            pltpu.make_async_remote_copy(
                src_ref=parts.at[target],
                dst_ref=got_parts.at[d - 1],
                send_sem=part_send.at[d - 1],
                recv_sem=part_recv.at[d - 1],
                device_id=others[d - 1],
                device_id_type=MESH,
            )
        )
        copies[-1].start()
    partial_of(row)
    for copy in copies:
        copy.wait()
    blocks = [parts[row]] + [got_parts[d] for d in range(row_count - 1)]
    levels = [
        jnp.sum(block[:, channels : channels + 128].astype(f32), axis=1, keepdims=True)
        for block in blocks
    ]
    top = functools.reduce(jnp.maximum, levels)
    weights = [jnp.exp2(level - top) for level in levels]
    total = functools.reduce(jnp.add, weights)
    mean = functools.reduce(
        jnp.add, [w * block[:, 0:channels].astype(f32) for w, block in zip(weights, blocks)]
    )
    mean = (mean / total).astype(bf16)
    attention = times(mean, value_weight[...]).astype(bf16)
    projected = times(attention, out_weight[...])
    mixed = (tokens[...].astype(f32) + projected).astype(bf16).astype(f32)
    flat[...] = silu(rms_scale(mixed, gain_one[...][None, :]))
    small[...] = jnp.zeros_like(small)
    for r in range(height):
        small[r, 0:width, :] = flat[r * width : (r + 1) * width, :]
    frame = small[...]
    put_pieces(frame, small[jnp.maximum(tall, 1) - 1], 0, tall, wide, sent_one)
    halos = halo_copies(counts, sent_one, got_one, send_sems.at[0], recv_sems.at[0])
    for copy in halos:
        copy.start()
    load.wait()
    for copy in halos:
        copy.wait()
    extend(frame, 0, tall, wide, got_one, counts, shifted_one)
    size = height * breadth
    y_one = sum_one[...] + convolve_rows(shifted_one, 1, held_one, times, 0, size, breadth)
    y_one = y_one.astype(bf16).astype(f32)
    small[...] = silu(rms_scale(y_one, gain_two[...][None, :])).reshape(height, breadth, channels)
    frame = small[...]
    put_pieces(frame, small[jnp.maximum(tall, 1) - 1], 0, tall, wide, sent_two)
    halos = halo_copies(counts, sent_two, got_two, send_sems.at[1], recv_sems.at[1])
    for copy in halos:
        copy.start()
    for copy in halos:
        copy.wait()
    extend(frame, 0, tall, wide, got_two, counts, shifted_two)
    for p in range(2):
        for q in range(2):
            phase = jnp.zeros((size, conv_two.shape[1]), f32)
            for a in range(2):
                for b in range(2):
                    first = (p + a) * breadth
                    phase += times_t(
                        shifted_two[0, q + b, first : first + size, :],
                        conv_two[p * 8 + q * 4 + a * 2 + b],
                    )
            for i in range(height):
                for lane in range(fine_sum.shape[0]):
                    fine_sum[lane, 2 * i + p, pl.ds(q, breadth, stride=2), :] = phase[
                        i * breadth : (i + 1) * breadth, lane * 128 : (lane + 1) * 128
                    ]
    fine_height, fine_narrow, channels_out = out.shape
    fine_breadth = sum_two.shape[1]
    fine_cols = lax.broadcasted_iota(jnp.int32, (fine_narrow, channels_out), 0)
    for i in range(fine_height):
        keep = jnp.logical_and(fine_cols < 2 * wide, i < 2 * tall)
        for lane in range(fine_sum.shape[0]):
            place = slice(lane * 128, min(lane * 128 + 128, channels_out))
            count = place.stop - place.start
            line = fine_sum[lane, i, 0:fine_narrow, 0:count] + sum_two[i, 0:fine_narrow, place]
            out[i, :, place] = jnp.where(keep[:, place], line, 0.0).astype(bf16)


def remote_call(kernel, out_shape, kinds, scratch, number, flops):
    return pl.pallas_call(
        kernel,
        out_shape=out_shape,
        in_specs=[pl.BlockSpec(memory_space=kind) for kind in kinds],
        out_specs=jax.tree.map(lambda _: pl.BlockSpec(memory_space=pltpu.VMEM), out_shape),
        scratch_shapes=scratch,
        compiler_params=pltpu.CompilerParams(
            collective_id=number, has_side_effects=True, vmem_limit_bytes=vmem_bytes
        ),
        cost_estimate=pl.CostEstimate(flops=flops, bytes_accessed=20_000_000, transcendentals=0),
    )


def local(
    counts, tokens, row_sizes, col_sizes, norm_gain, query_weight, key_weight, value_weight,
    out_weight, cache_one, gain_one, conv_one, cache_two, gain_two, conv_two,
):
    height, width, channels = tokens.shape
    channels_out = conv_two.shape[-1]
    rows, cols = counts
    breadth = round_up(width + 1, 16)
    fine_breadth = round_up(2 * width + 1, 16)
    each = round_up(height * width, 16)

    flat = jnp.pad(tokens.reshape(height * width, channels), ((0, each - height * width), (0, 0)))
    wide_one = jnp.pad(cache_one, ((0, 0), (0, 0), (0, breadth - width), (0, 0)))
    kernels_one = conv_one.reshape(27, channels, channels)
    kernels_two = jnp.swapaxes(conv_two, 3, 4).reshape(27, channels_out, channels)
    line_one = max(breadth, round_up(height, 16))
    line_two = max(fine_breadth, round_up(2 * height, 16))
    lanes_out = round_up(channels_out, 128)
    fast = fast_part(cols)
    slow = cols // fast
    vm, sm, dma = pltpu.VMEM, pltpu.SMEM, pltpu.SemaphoreType.DMA
    shape = jax.ShapeDtypeStruct
    sum_one, sum_two, keys, queries, phase_weights = remote_call(
        functools.partial(prior_kernel, counts),
        (
            shape((height * breadth, channels), f32),
            shape((2 * height * fine_breadth, channels_out), f32),
            shape((cols, each, channels), bf16),
            shape((rows, each, channels), bf16),
            shape((16, lanes_out, channels), bf16),
        ),
        [sm] * 2 + [vm] * 6 + [pl.ANY] * 2,
        [
            vm((8, 2, line_one, channels), bf16),
            vm((8, 2, line_one, channels), bf16),
            vm((8, 2, line_two, channels), bf16),
            vm((8, 2, line_two, channels), bf16),
            vm((2, 3, (height + 2) * breadth, channels), bf16),
            vm((2, 3, (2 * height + 2) * fine_breadth, channels), bf16),
            vm((18, channels, channels), bf16),
            vm((27, channels_out, channels), bf16),
            dma((2, 8)),
            dma((2, 8)),
            dma((rows - 1,)),
            dma((rows - 1,)),
            dma((slow,)),
            dma((slow,)),
            dma((max(fast - 1, 1), slow)),
            dma((cols,)),
            dma((2,)),
        ],
        1,
        9_000_000_000,
    )(
        row_sizes, col_sizes, flat, norm_gain, query_weight, key_weight,
        wide_one, cache_two, kernels_one, kernels_two,
    )
    sum_two = sum_two.reshape(2 * height, fine_breadth, channels_out)
    return remote_call(
        functools.partial(tail_kernel, counts, width),
        shape((2 * height, 2 * width, channels_out), bf16),
        [sm] * 2 + [vm] * 10 + [pl.ANY],
        [
            vm((rows, each, channels + 128), bf16),
            vm((round_up(cols, 8), each), f32),
            vm((9, channels, channels), bf16),
            vm((rows - 1, each, channels + 128), bf16),
            vm((8, 1, line_one, channels), bf16),
            vm((8, 1, line_one, channels), bf16),
            vm((8, 1, line_one, channels), bf16),
            vm((8, 1, line_one, channels), bf16),
            vm((1, 3, (height + 2) * breadth, channels), bf16),
            vm((1, 3, (height + 2) * breadth, channels), bf16),
            vm((each, channels), f32),
            vm((height, breadth, channels), f32),
            vm((lanes_out // 128, 2 * height, 2 * breadth, 128), f32),
            dma((rows - 1,)),
            dma((rows - 1,)),
            dma((2, 8)),
            dma((2, 8)),
            dma,
        ],
        2,
        9_000_000_000,
    )(
        row_sizes, col_sizes, queries, keys, flat, value_weight, out_weight,
        gain_one, gain_two, sum_one, sum_two, phase_weights, kernels_one,
    )


def solution(mesh):
    tiled = P("row", "col", None)
    framed = P(None, "row", "col", None)
    placed = (tiled,) + (P(),) * 7 + (framed, P(), P(), framed, P(), P())
    counts = (mesh.shape["row"], mesh.shape["col"])
    return jax.shard_map(
        functools.partial(local, counts),
        mesh=mesh,
        in_specs=placed,
        out_specs=P("row", "col", None),
        check_vma=False,
    )
```

```python
import functools
import math

import jax
import jax.numpy as jnp
from jax import lax
from jax.experimental import pallas as pl
from jax.experimental.pallas import tpu as pltpu
from jax.sharding import PartitionSpec as P

epsilon = 1e-06
masked_score = -1e30
f32 = jnp.float32
bf16 = jnp.bfloat16
MESH = pl.DeviceIdType.MESH
steps = ((-1, 0), (1, 0), (0, -1), (0, 1), (-1, -1), (-1, 1), (1, -1), (1, 1))
vmem_bytes = 58 * 1024 * 1024


def round_up(value, unit):
    return -(-value // unit) * unit


def rms_scale(wide, gain_vec):
    return wide * lax.rsqrt(jnp.mean(wide * wide, axis=-1, keepdims=True) + epsilon) * gain_vec


def silu(wide):
    return wide / (1.0 + jnp.exp(-wide))


def times(left, right):
    return jnp.dot(left, right, preferred_element_type=f32)


def times_t(left, right):
    return lax.dot_general(left, right, (((1,), (1,)), ((), ())), preferred_element_type=f32)


def wrapped(position, step, count):
    return lax.rem(position + step + count, count)


def partner(counts, step):
    return (
        wrapped(lax.axis_index("row"), step[0], counts[0]),
        wrapped(lax.axis_index("col"), step[1], counts[1]),
    )


def greet(devices):
    barrier = pltpu.get_barrier_semaphore()
    for device in devices:
        pl.semaphore_signal(barrier, inc=1, device_id=device, device_id_type=MESH)
    pl.semaphore_wait(barrier, len(devices))


def iota3(shape, dim):
    return lax.broadcasted_iota(jnp.int32, shape, dim)


def halo_copies(counts, lengths, sent, got, send_sems, recv_sems):
    def piece(ref, k):
        return ref.at[k, :, 0 : lengths[0 if k < 2 else (1 if k < 4 else 2)], :]

    return [
        pltpu.make_async_remote_copy(
            src_ref=piece(sent, k),
            dst_ref=piece(got, k),
            send_sem=send_sems.at[k],
            recv_sem=recv_sems.at[k],
            device_id=partner(counts, step),
            device_id_type=MESH,
        )
        for k, step in enumerate(steps)
    ]


def put_pieces(frame, last_line, f, tall, wide, sent):
    height, breadth, channels = frame.shape
    cols = iota3(frame.shape, 1)
    left = jnp.concatenate([frame[r, 0:1, :] for r in range(height)], axis=0)
    right = jnp.sum(jnp.where(cols == wide - 1, frame, 0.0), axis=1)
    side_rows = iota3(left.shape, 0)
    sent[0, f, 0:breadth, :] = frame[0].astype(bf16)
    sent[1, f, 0:breadth, :] = last_line.astype(bf16)
    sent[2, f, 0:height, :] = left.astype(bf16)
    sent[3, f, 0:height, :] = right.astype(bf16)
    for k, side in ((4, left), (5, right)):
        sent[k, f, 0:16, :] = jnp.broadcast_to(side[0:1], (16, channels)).astype(bf16)
        low = jnp.sum(jnp.where(side_rows == tall - 1, side, 0.0), axis=0, keepdims=True)
        sent[k + 2, f, 0:16, :] = jnp.broadcast_to(low, (16, channels)).astype(bf16)


def extend(frame, f, tall, wide, got, counts, shifted):
    height, breadth, channels = frame.shape
    row, col = lax.axis_index("row"), lax.axis_index("col")

    def piece(k, count):
        ok = None
        step = steps[k]
        if step[0] != 0:
            ok = (row > 0) if step[0] > 0 else (row < counts[0] - 1)
        if step[1] != 0:
            ok_col = (col > 0) if step[1] > 0 else (col < counts[1] - 1)
            ok = ok_col if ok is None else jnp.logical_and(ok, ok_col)
        return got[k, f, 0 : round_up(count, 16), :].astype(f32) * jnp.where(ok, 1.0, 0.0)

    below, above = piece(0, breadth), piece(1, breadth)
    right_side, left_side = piece(2, height), piece(3, height)
    right_low, left_low = piece(4, 1)[0:1], piece(5, 1)[0:1]
    right_top, left_top = piece(6, 1)[0:1], piece(7, 1)[0:1]
    line_cols = iota3((breadth, channels), 0)
    below = jnp.where(line_cols == wide, right_low, below)
    above = jnp.where(line_cols == wide, right_top, above)
    size = (height + 2) * breadth
    for r in range(height + 2):
        if r == 0:
            line, first = above, left_top
        else:
            if r <= height:
                line = jnp.where(line_cols == wide, right_side[r - 1 : r], frame[r - 1])
                first = left_side[r - 1 : r]
                line = jnp.where(tall + 1 == r, below, line)
                first = jnp.where(tall + 1 == r, left_low, first)
            else:
                line, first = below, left_low
        before = jnp.where(line_cols == 0, first, pltpu.roll(line, 1, 0))
        after = pltpu.roll(line, breadth - 1, 0)
        place = slice(r * breadth, (r + 1) * breadth)
        shifted[f, 0, place, :] = before.astype(bf16)
        shifted[f, 1, place, :] = line.astype(bf16)
        shifted[f, 2, place, :] = after.astype(bf16)


def widened(frame, breadth):
    frame = frame.astype(f32)
    gap = breadth - frame.shape[-2]
    if gap == 0:
        return frame
    zeros = jnp.zeros(frame.shape[:-2] + (gap, frame.shape[-1]), f32)
    return jnp.concatenate([frame, zeros], axis=-2)


def key_spread(counts, keys, sems):
    fwd_sems, bwd_sems, fast_sems, recv_sems = sems
    cols = counts[1]
    fast = fast_part(cols)
    slow = cols // fast
    row, col = lax.axis_index("row"), lax.axis_index("col")
    s, f = col // fast, col % fast

    def copy_to(block, sem, slow_at, fast_at):
        return pltpu.make_async_remote_copy(
            src_ref=keys.at[block],
            dst_ref=keys.at[block],
            send_sem=sem,
            recv_sem=recv_sems.at[block],
            device_id=(row, slow_at * fast + fast_at),
            device_id_type=MESH,
        )

    def fast_copies(block_s):
        return [
            copy_to(block_s * fast + f, fast_sems.at[d - 1, block_s], s, (f + d) % fast)
            for d in range(1, fast)
        ]

    def line_copy(hop, up):
        block_s = s - hop if up else s + hop
        sems_at = fwd_sems if up else bwd_sems
        return copy_to(block_s * fast + f, sems_at.at[hop], s + 1 if up else s - 1, f)

    def goes(hop, up):
        if up:
            return jnp.logical_and(s - hop >= 0, s + 1 < slow)
        return jnp.logical_and(s + hop < slow, s - 1 >= 0)

    def start():
        for up in (True, False):
            @pl.when(goes(0, up))
            def _():
                line_copy(0, up).start()

        for copy in fast_copies(s):
            copy.start()

    def hop(step):
        for up in (True, False):
            came = (s - step >= 0) if up else (s + step < slow)

            @pl.when(came)
            def _():
                block_s = s - step if up else s + step
                copy_to(block_s * fast + f, fwd_sems.at[0], s, f).wait_recv()
                for copy in fast_copies(block_s):
                    copy.start()

            if step < slow - 1:
                @pl.when(goes(step, up))
                def _():
                    line_copy(step, up).start()

    def finish():
        for block_s in range(slow):
            for d in range(1, fast):
                copy_to(block_s * fast + (f + d) % fast, fwd_sems.at[0], s, f).wait_recv()
            for copy in fast_copies(block_s):
                copy.wait_send()
        for step in range(slow - 1):
            for up in (True, False):
                @pl.when(goes(step, up))
                def _():
                    line_copy(step, up).wait_send()

    greeted = [(row, s * fast + (f + d) % fast) for d in range(1, fast)]
    return start, hop, finish, greeted, slow


def fast_part(cols):
    fast = 1 << ((cols.bit_length() - 1) // 2)
    return fast if cols % fast == 0 else 1


def convolve_rows(shifted, frames, conv, product, start, size, breadth, first=0):
    part = None
    for f in range(frames):
        for a in range(3):
            for b in range(3):
                rows = shifted[f, b, start + a * breadth : start + a * breadth + size, :]
                term = product(rows, conv[first + f * 9 + a * 3 + b])
                part = term if part is None else part + term
    return part


def whole_kernel(
    counts, width, row_sizes, col_sizes, tokens, norm_gain, query_weight, key_weight, value_weight,
    out_weight, cache_one, gain_one, cache_two, gain_two, conv_one, conv_two, out,
    sum_one, sum_two, keys, queries, phase_weights, parts, got_parts, bias, flat, small, fine_sum,
    sent_one, got_one, sent_two, got_two, sent_new, got_new, sent_last, got_last,
    shifted_one, shifted_two, shifted_new, shifted_last, held_one, held_two,
    send_sems, recv_sems, query_send, query_recv, fwd_sems, bwd_sems, fast_sems, key_recv, load_sems,
    part_send, part_recv,
):
    row_count, col_count = counts
    row, col = lax.axis_index("row"), lax.axis_index("col")
    tall, wide = row_sizes[row], col_sizes[col]
    loads = [
        pltpu.make_async_copy(conv_two, held_two, load_sems.at[0]),
        pltpu.make_async_copy(conv_one, held_one, load_sems.at[1]),
    ]
    for load in loads:
        load.start()
    key_sems = (fwd_sems, bwd_sems, fast_sems, key_recv)
    start, hop, finish, fast_others, slow = key_spread(counts, keys, key_sems)
    fast = col_count // slow
    line = [
        (row, wrapped(col, step * fast, col_count)) for step in ((1, -1) if slow > 1 else ())
    ]
    others = [(wrapped(row, d, row_count), col) for d in range(1, row_count)]
    greet(
        others + fast_others + line
        + [partner(counts, step) for step in steps if step[1] != 0]
    )
    normed = rms_scale(tokens[...].astype(f32), norm_gain[...][None, :]).astype(bf16)
    keys[col] = normed
    start()
    query = times(normed, query_weight[...]).astype(bf16)
    unit = math.log2(math.e) / math.sqrt(tokens.shape[1])
    queries[row] = (times_t(query, key_weight[...]) * unit).astype(bf16)
    query_copies = [
        pltpu.make_async_remote_copy(
            src_ref=queries.at[row],
            dst_ref=queries.at[row],
            send_sem=query_send.at[d],
            recv_sem=query_recv.at[d],
            device_id=device,
            device_id_type=MESH,
        )
        for d, device in enumerate(others)
    ]
    for copy in query_copies:
        copy.start()
    breadth, fine_breadth = cache_one.shape[2], round_up(cache_two.shape[2] + 1, 16)
    height = cache_one.shape[1]
    lengths_one = (breadth, round_up(height, 16), 16)
    lengths_two = (fine_breadth, round_up(2 * height, 16), 16)
    for f in range(2):
        last_line = cache_one[f, jnp.maximum(tall, 1) - 1].astype(f32)
        put_pieces(cache_one[f].astype(f32), last_line, f, tall, wide, sent_one)
    halos_one = halo_copies(counts, lengths_one, sent_one, got_one, send_sems.at[0], recv_sems.at[0])
    for copy in halos_one:
        copy.start()
    for f in range(2):
        last_line = widened(cache_two[f, 2 * jnp.maximum(tall, 1) - 1], fine_breadth)
        frame = widened(cache_two[f], fine_breadth)
        put_pieces(frame, last_line, f, 2 * tall, 2 * wide, sent_two)
    halos_two = halo_copies(counts, lengths_two, sent_two, got_two, send_sems.at[1], recv_sems.at[1])
    for copy in halos_two:
        copy.start()
    if slow > 1:
        hop(1)
    loads[0].wait()
    channels_out = held_two.shape[1]
    phase_weights[:, channels_out:, :] = jnp.zeros_like(phase_weights[:, channels_out:, :])
    for p in range(2):
        for q in range(2):
            for a in range(2):
                for b in range(2):
                    rows_in = ((0,), (1, 2))[a] if p == 0 else ((0, 1), (2,))[a]
                    cols_in = ((0,), (1, 2))[b] if q == 0 else ((0, 1), (2,))[b]
                    taps = [held_two[18 + 3 * i + j].astype(f32) for i in rows_in for j in cols_in]
                    total = functools.reduce(jnp.add, taps).astype(bf16)
                    phase_weights[p * 8 + q * 4 + a * 2 + b, 0:channels_out, :] = total
    for copy in halos_one:
        copy.wait()
    for f in range(2):
        extend(cache_one[f].astype(f32), f, tall, wide, got_one, counts, shifted_one)
    if slow > 2:
        hop(2)
    loads[1].wait()
    sum_one[...] = convolve_rows(
        shifted_one, 2, held_one, times, 0, sum_one.shape[0], breadth
    )
    for step in range(3, slow):
        hop(step)
    for copy in halos_two:
        copy.wait()
    for f in range(2):
        frame = widened(cache_two[f], fine_breadth)
        extend(frame, f, 2 * tall, 2 * wide, got_two, counts, shifted_two)
    fine_total = sum_two.shape[0]
    fine_chunk = fine_total // 3 if fine_total % 48 == 0 else fine_total

    def prior_two(part):
        at = part * fine_chunk
        if at < fine_total:
            sum_two[at : at + fine_chunk, :] = convolve_rows(
                shifted_two, 2, held_two, times_t, at, fine_chunk, fine_breadth
            )

    prior_two(0)
    finish()
    for copy in query_copies:
        copy.wait()
    each, channels = tokens.shape
    slot = lax.broadcasted_iota(jnp.int32, (1, each), 1)
    slot_row = jnp.zeros((1, each), jnp.int32)
    for r in range(1, height + 1):
        slot_row += jnp.where(slot >= r * width, 1, 0)
    slot_col = slot - slot_row * width
    for c in range(col_count):
        usable = jnp.logical_and(slot_row < tall, slot_col < col_sizes[c])
        bias[c : c + 1, :] = jnp.where(usable, 0.0, masked_score)
    masks = jnp.concatenate([bias[c : c + 1, :] for c in range(col_count)], axis=1)
    lanes = lax.broadcasted_iota(jnp.int32, (each, 128), 1)

    def partial_of(target):
        all_keys = keys[...].reshape(col_count * each, channels)
        scores = times_t(queries[target], all_keys) + masks
        highest = jnp.max(scores, axis=1, keepdims=True)
        expos = jnp.exp2(scores - highest)
        total = jnp.sum(expos, axis=1, keepdims=True)
        mean = times(expos.astype(bf16), all_keys) / total
        level = highest + jnp.log2(total)
        high = level.astype(bf16).astype(f32)
        mid = (level - high).astype(bf16).astype(f32)
        low = level - high - mid
        coded = jnp.where(lanes == 0, high, jnp.where(lanes == 1, mid, jnp.where(lanes == 2, low, 0.0)))
        parts[target, :, 0:channels] = mean.astype(bf16)
        parts[target, :, channels : channels + 128] = coded.astype(bf16)

    copies = []
    for d in sorted(range(1, row_count), key=lambda d: -min(d, row_count - d)):
        target = others[d - 1][0]
        partial_of(target)
        copies.append(
            pltpu.make_async_remote_copy(
                src_ref=parts.at[target],
                dst_ref=got_parts.at[d - 1],
                send_sem=part_send.at[d - 1],
                recv_sem=part_recv.at[d - 1],
                device_id=others[d - 1],
                device_id_type=MESH,
            )
        )
        copies[-1].start()
    partial_of(row)
    prior_two(1)
    for copy in copies:
        copy.wait()
    blocks = [parts[row]] + [got_parts[d] for d in range(row_count - 1)]
    levels = [
        jnp.sum(block[:, channels : channels + 128].astype(f32), axis=1, keepdims=True)
        for block in blocks
    ]
    top = functools.reduce(jnp.maximum, levels)
    weights = [jnp.exp2(level - top) for level in levels]
    total = functools.reduce(jnp.add, weights)
    mean = functools.reduce(
        jnp.add, [w * block[:, 0:channels].astype(f32) for w, block in zip(weights, blocks)]
    )
    mean = (mean / total).astype(bf16)
    attention = times(mean, value_weight[...]).astype(bf16)
    projected = times(attention, out_weight[...])
    mixed = (tokens[...].astype(f32) + projected).astype(bf16).astype(f32)
    flat[...] = silu(rms_scale(mixed, gain_one[...][None, :]))
    small[...] = jnp.zeros_like(small)
    for r in range(height):
        small[r, 0:width, :] = flat[r * width : (r + 1) * width, :]
    frame = small[...]
    put_pieces(frame, small[jnp.maximum(tall, 1) - 1], 0, tall, wide, sent_new)
    halos = halo_copies(counts, lengths_one, sent_new, got_new, send_sems.at[2], recv_sems.at[2])
    for copy in halos:
        copy.start()
    prior_two(2)
    for copy in halos:
        copy.wait()
    extend(frame, 0, tall, wide, got_new, counts, shifted_new)
    size_one = height * breadth
    y_one = sum_one[...] + convolve_rows(shifted_new, 1, held_one, times, 0, size_one, breadth, 18)
    y_one = y_one.astype(bf16).astype(f32)
    small[...] = silu(rms_scale(y_one, gain_two[...][None, :])).reshape(height, breadth, channels)
    frame = small[...]
    put_pieces(frame, small[jnp.maximum(tall, 1) - 1], 0, tall, wide, sent_last)
    halos = halo_copies(counts, lengths_one, sent_last, got_last, send_sems.at[3], recv_sems.at[3])
    for copy in halos:
        copy.start()
    for copy in halos:
        copy.wait()
    extend(frame, 0, tall, wide, got_last, counts, shifted_last)
    for p in range(2):
        for q in range(2):
            phase = jnp.zeros((size_one, phase_weights.shape[1]), f32)
            for a in range(2):
                for b in range(2):
                    first = (p + a) * breadth
                    phase += times_t(
                        shifted_last[0, q + b, first : first + size_one, :],
                        phase_weights[p * 8 + q * 4 + a * 2 + b],
                    )
            for i in range(height):
                for lane in range(fine_sum.shape[0]):
                    fine_sum[lane, 2 * i + p, pl.ds(q, breadth, stride=2), :] = phase[
                        i * breadth : (i + 1) * breadth, lane * 128 : (lane + 1) * 128
                    ]
    fine_height, fine_narrow, channels_out = out.shape
    fine_cols = lax.broadcasted_iota(jnp.int32, (fine_narrow, channels_out), 0)
    for i in range(fine_height):
        keep = jnp.logical_and(fine_cols < 2 * wide, i < 2 * tall)
        for lane in range(fine_sum.shape[0]):
            place = slice(lane * 128, min(lane * 128 + 128, channels_out))
            count = place.stop - place.start
            line = fine_sum[lane, i, 0:fine_narrow, 0:count] + sum_two[i * fine_breadth : i * fine_breadth + fine_narrow, place]
            out[i, :, place] = jnp.where(keep[:, place], line, 0.0).astype(bf16)


def remote_call(kernel, out_shape, kinds, scratch, number, flops):
    return pl.pallas_call(
        kernel,
        out_shape=out_shape,
        in_specs=[pl.BlockSpec(memory_space=kind) for kind in kinds],
        out_specs=jax.tree.map(lambda _: pl.BlockSpec(memory_space=pltpu.VMEM), out_shape),
        scratch_shapes=scratch,
        compiler_params=pltpu.CompilerParams(
            collective_id=number, has_side_effects=True, vmem_limit_bytes=vmem_bytes
        ),
        cost_estimate=pl.CostEstimate(flops=flops, bytes_accessed=20_000_000, transcendentals=0),
    )


def local(
    counts, tokens, row_sizes, col_sizes, norm_gain, query_weight, key_weight, value_weight,
    out_weight, cache_one, gain_one, conv_one, cache_two, gain_two, conv_two,
):
    height, width, channels = tokens.shape
    channels_out = conv_two.shape[-1]
    rows, cols = counts
    breadth = round_up(width + 1, 16)
    fine_breadth = round_up(2 * width + 1, 16)
    each = round_up(height * width, 16)

    flat = jnp.pad(tokens.reshape(height * width, channels), ((0, each - height * width), (0, 0)))
    wide_one = jnp.pad(cache_one, ((0, 0), (0, 0), (0, breadth - width), (0, 0)))
    kernels_one = conv_one.reshape(27, channels, channels)
    kernels_two = jnp.swapaxes(conv_two, 3, 4).reshape(27, channels_out, channels)
    line_one = max(breadth, round_up(height, 16))
    line_two = max(fine_breadth, round_up(2 * height, 16))
    lanes_out = round_up(channels_out, 128)
    fast = fast_part(cols)
    slow = cols // fast
    vm, sm, dma = pltpu.VMEM, pltpu.SMEM, pltpu.SemaphoreType.DMA
    shape = jax.ShapeDtypeStruct
    return remote_call(
        functools.partial(whole_kernel, counts, width),
        shape((2 * height, 2 * width, channels_out), bf16),
        [sm] * 2 + [vm] * 10 + [pl.ANY] * 2,
        [
            vm((height * breadth, channels), f32),
            vm((2 * height * fine_breadth, channels_out), f32),
            vm((cols, each, channels), bf16),
            vm((rows, each, channels), bf16),
            vm((16, lanes_out, channels), bf16),
            vm((rows, each, channels + 128), bf16),
            vm((rows - 1, each, channels + 128), bf16),
            vm((round_up(cols, 8), each), f32),
            vm((each, channels), f32),
            vm((height, breadth, channels), f32),
            vm((lanes_out // 128, 2 * height, 2 * breadth, 128), f32),
            vm((8, 2, line_one, channels), bf16),
            vm((8, 2, line_one, channels), bf16),
            vm((8, 2, line_two, channels), bf16),
            vm((8, 2, line_two, channels), bf16),
            vm((8, 1, line_one, channels), bf16),
            vm((8, 1, line_one, channels), bf16),
            vm((8, 1, line_one, channels), bf16),
            vm((8, 1, line_one, channels), bf16),
            vm((2, 3, (height + 2) * breadth, channels), bf16),
            vm((2, 3, (2 * height + 2) * fine_breadth, channels), bf16),
            vm((1, 3, (height + 2) * breadth, channels), bf16),
            vm((1, 3, (height + 2) * breadth, channels), bf16),
            vm((27, channels, channels), bf16),
            vm((27, channels_out, channels), bf16),
            dma((4, 8)),
            dma((4, 8)),
            dma((rows - 1,)),
            dma((rows - 1,)),
            dma((slow,)),
            dma((slow,)),
            dma((max(fast - 1, 1), slow)),
            dma((cols,)),
            dma((2,)),
            dma((rows - 1,)),
            dma((rows - 1,)),
        ],
        1,
        18_000_000_000,
    )(
        row_sizes, col_sizes, flat, norm_gain, query_weight, key_weight, value_weight, out_weight,
        wide_one, gain_one, cache_two, gain_two, kernels_one, kernels_two,
    )


def solution(mesh):
    tiled = P("row", "col", None)
    framed = P(None, "row", "col", None)
    placed = (tiled,) + (P(),) * 7 + (framed, P(), P(), framed, P(), P())
    counts = (mesh.shape["row"], mesh.shape["col"])
    return jax.shard_map(
        functools.partial(local, counts),
        mesh=mesh,
        in_specs=placed,
        out_specs=P("row", "col", None),
        check_vma=False,
    )
```

```python
import functools
import math

import jax
import jax.numpy as jnp
from jax import lax
from jax.experimental import pallas as pl
from jax.experimental.pallas import tpu as pltpu
from jax.sharding import PartitionSpec as P

epsilon = 1e-06
masked_score = -1e30
f32 = jnp.float32
bf16 = jnp.bfloat16
MESH = pl.DeviceIdType.MESH
steps = ((-1, 0), (1, 0), (0, -1), (0, 1), (-1, -1), (-1, 1), (1, -1), (1, 1))
vmem_bytes = 58 * 1024 * 1024


def round_up(value, unit):
    return -(-value // unit) * unit


def rms_scale(wide, gain_vec):
    return wide * lax.rsqrt(jnp.mean(wide * wide, axis=-1, keepdims=True) + epsilon) * gain_vec


def silu(wide):
    return wide / (1.0 + jnp.exp(-wide))


def times(left, right):
    return jnp.dot(left, right, preferred_element_type=f32)


def times_t(left, right):
    return lax.dot_general(left, right, (((1,), (1,)), ((), ())), preferred_element_type=f32)


def wrapped(position, step, count):
    return lax.rem(position + step + count, count)


def partner(counts, step):
    return (
        wrapped(lax.axis_index("row"), step[0], counts[0]),
        wrapped(lax.axis_index("col"), step[1], counts[1]),
    )


def greet(devices):
    barrier = pltpu.get_barrier_semaphore()
    for device in devices:
        pl.semaphore_signal(barrier, inc=1, device_id=device, device_id_type=MESH)
    return lambda: pl.semaphore_wait(barrier, len(devices))


def iota3(shape, dim):
    return lax.broadcasted_iota(jnp.int32, shape, dim)


def halo_copies(counts, lengths, sent, got, send_sems, recv_sems):
    def piece(ref, k):
        return ref.at[k, :, 0 : lengths[0 if k < 2 else (1 if k < 4 else 2)], :]

    return [
        pltpu.make_async_remote_copy(
            src_ref=piece(sent, k),
            dst_ref=piece(got, k),
            send_sem=send_sems.at[k],
            recv_sem=recv_sems.at[k],
            device_id=partner(counts, step),
            device_id_type=MESH,
        )
        for k, step in enumerate(steps)
    ]


def put_pieces(frame, last_line, f, tall, wide, sent):
    height, breadth, channels = frame.shape
    cols = iota3(frame.shape, 1)
    left = jnp.concatenate([frame[r, 0:1, :] for r in range(height)], axis=0)
    right = jnp.sum(jnp.where(cols == wide - 1, frame, 0.0), axis=1)
    side_rows = iota3(left.shape, 0)
    sent[0, f, 0:breadth, :] = frame[0].astype(bf16)
    sent[1, f, 0:breadth, :] = last_line.astype(bf16)
    sent[2, f, 0:height, :] = left.astype(bf16)
    sent[3, f, 0:height, :] = right.astype(bf16)
    for k, side in ((4, left), (5, right)):
        sent[k, f, 0:16, :] = jnp.broadcast_to(side[0:1], (16, channels)).astype(bf16)
        low = jnp.sum(jnp.where(side_rows == tall - 1, side, 0.0), axis=0, keepdims=True)
        sent[k + 2, f, 0:16, :] = jnp.broadcast_to(low, (16, channels)).astype(bf16)


def extend(frame, f, tall, wide, got, counts, shifted):
    height, breadth, channels = frame.shape
    row, col = lax.axis_index("row"), lax.axis_index("col")

    def piece(k, count):
        ok = None
        step = steps[k]
        if step[0] != 0:
            ok = (row > 0) if step[0] > 0 else (row < counts[0] - 1)
        if step[1] != 0:
            ok_col = (col > 0) if step[1] > 0 else (col < counts[1] - 1)
            ok = ok_col if ok is None else jnp.logical_and(ok, ok_col)
        return got[k, f, 0 : round_up(count, 16), :].astype(f32) * jnp.where(ok, 1.0, 0.0)

    below, above = piece(0, breadth), piece(1, breadth)
    right_side, left_side = piece(2, height), piece(3, height)
    right_low, left_low = piece(4, 1)[0:1], piece(5, 1)[0:1]
    right_top, left_top = piece(6, 1)[0:1], piece(7, 1)[0:1]
    line_cols = iota3((breadth, channels), 0)
    below = jnp.where(line_cols == wide, right_low, below)
    above = jnp.where(line_cols == wide, right_top, above)
    size = (height + 2) * breadth
    for r in range(height + 2):
        if r == 0:
            line, first = above, left_top
        else:
            if r <= height:
                line = jnp.where(line_cols == wide, right_side[r - 1 : r], frame[r - 1])
                first = left_side[r - 1 : r]
                line = jnp.where(tall + 1 == r, below, line)
                first = jnp.where(tall + 1 == r, left_low, first)
            else:
                line, first = below, left_low
        before = jnp.where(line_cols == 0, first, pltpu.roll(line, 1, 0))
        after = pltpu.roll(line, breadth - 1, 0)
        place = slice(r * breadth, (r + 1) * breadth)
        shifted[f, 0, place, :] = before.astype(bf16)
        shifted[f, 1, place, :] = line.astype(bf16)
        shifted[f, 2, place, :] = after.astype(bf16)


def widened(frame, breadth):
    frame = frame.astype(f32)
    gap = breadth - frame.shape[-2]
    if gap == 0:
        return frame
    zeros = jnp.zeros(frame.shape[:-2] + (gap, frame.shape[-1]), f32)
    return jnp.concatenate([frame, zeros], axis=-2)


def key_spread(counts, keys, sems):
    fwd_sems, bwd_sems, fast_sems, recv_sems = sems
    cols = counts[1]
    fast = fast_part(cols)
    slow = cols // fast
    row, col = lax.axis_index("row"), lax.axis_index("col")
    s, f = col // fast, col % fast

    def copy_to(block, sem, slow_at, fast_at):
        return pltpu.make_async_remote_copy(
            src_ref=keys.at[block],
            dst_ref=keys.at[block],
            send_sem=sem,
            recv_sem=recv_sems.at[block],
            device_id=(row, slow_at * fast + fast_at),
            device_id_type=MESH,
        )

    def fast_copies(block_s):
        return [
            copy_to(block_s * fast + f, fast_sems.at[d - 1, block_s], s, (f + d) % fast)
            for d in range(1, fast)
        ]

    def line_copy(hop, up):
        block_s = s - hop if up else s + hop
        sems_at = fwd_sems if up else bwd_sems
        return copy_to(block_s * fast + f, sems_at.at[hop], s + 1 if up else s - 1, f)

    def goes(hop, up):
        if up:
            return jnp.logical_and(s - hop >= 0, s + 1 < slow)
        return jnp.logical_and(s + hop < slow, s - 1 >= 0)

    def start():
        for up in (True, False):
            @pl.when(goes(0, up))
            def _():
                line_copy(0, up).start()

        for copy in fast_copies(s):
            copy.start()

    def hop(step):
        for up in (True, False):
            came = (s - step >= 0) if up else (s + step < slow)

            @pl.when(came)
            def _():
                block_s = s - step if up else s + step
                copy_to(block_s * fast + f, fwd_sems.at[0], s, f).wait_recv()
                for copy in fast_copies(block_s):
                    copy.start()

            if step < slow - 1:
                @pl.when(goes(step, up))
                def _():
                    line_copy(step, up).start()

    def finish():
        for block_s in range(slow):
            for d in range(1, fast):
                copy_to(block_s * fast + (f + d) % fast, fwd_sems.at[0], s, f).wait_recv()
            for copy in fast_copies(block_s):
                copy.wait_send()
        for step in range(slow - 1):
            for up in (True, False):
                @pl.when(goes(step, up))
                def _():
                    line_copy(step, up).wait_send()

    greeted = [(row, s * fast + (f + d) % fast) for d in range(1, fast)]
    return start, hop, finish, greeted, slow


def fast_part(cols):
    fast = 1 << ((cols.bit_length() - 1) // 2)
    return fast if cols % fast == 0 else 1


def convolve_rows(shifted, frames, conv, product, start, size, breadth, first=0):
    part = None
    for f in range(frames):
        for a in range(3):
            for b in range(3):
                rows = shifted[f, b, start + a * breadth : start + a * breadth + size, :]
                term = product(rows, conv[first + f * 9 + a * 3 + b])
                part = term if part is None else part + term
    return part


def whole_kernel(
    counts, row_sizes, col_sizes, tokens, norm_gain, query_weight, key_weight, value_weight,
    out_weight, cache_one, gain_one, cache_two, gain_two, conv_one, conv_two, out,
    sum_one, sum_two, keys, queries, phase_weights, parts, got_parts, bias, flat, small, wide_one, fine_sum,
    sent_one, got_one, sent_two, got_two, sent_new, got_new, sent_last, got_last,
    shifted_one, shifted_two, shifted_new, shifted_last, held_one, held_two,
    send_sems, recv_sems, query_send, query_recv, fwd_sems, bwd_sems, fast_sems, key_recv, load_sems,
    part_send, part_recv,
):
    row_count, col_count = counts
    row, col = lax.axis_index("row"), lax.axis_index("col")
    tall, wide = row_sizes[row], col_sizes[col]
    loads = [
        pltpu.make_async_copy(conv_two, held_two, load_sems.at[0]),
        pltpu.make_async_copy(conv_one, held_one, load_sems.at[1]),
    ]
    for load in loads:
        load.start()
    key_sems = (fwd_sems, bwd_sems, fast_sems, key_recv)
    start, hop, finish, fast_others, slow = key_spread(counts, keys, key_sems)
    fast = col_count // slow
    line = [
        (row, wrapped(col, step * fast, col_count)) for step in ((1, -1) if slow > 1 else ())
    ]
    others = [(wrapped(row, d, row_count), col) for d in range(1, row_count)]
    greeted = greet(
        others + fast_others + line
        + [partner(counts, step) for step in steps if step[1] != 0]
    )
    height, width, channels = tokens.shape
    each = flat.shape[0]
    for r in range(height):
        flat[r * width : (r + 1) * width, :] = tokens[r].astype(f32)
    if each > height * width:
        flat[height * width :, :] = jnp.zeros((each - height * width, channels), f32)
    normed = rms_scale(flat[...], norm_gain[...][None, :]).astype(bf16)
    keys[col] = normed
    query = times(normed, query_weight[...]).astype(bf16)
    unit = math.log2(math.e) / math.sqrt(channels)
    queries[row] = (times_t(query, key_weight[...]) * unit).astype(bf16)
    greeted()
    start()
    query_copies = [
        pltpu.make_async_remote_copy(
            src_ref=queries.at[row],
            dst_ref=queries.at[row],
            send_sem=query_send.at[d],
            recv_sem=query_recv.at[d],
            device_id=device,
            device_id_type=MESH,
        )
        for d, device in enumerate(others)
    ]
    for copy in query_copies:
        copy.start()
    breadth, fine_breadth = small.shape[1], round_up(cache_two.shape[2] + 1, 16)
    lengths_one = (breadth, round_up(height, 16), 16)
    lengths_two = (fine_breadth, round_up(2 * height, 16), 16)
    wide_one[...] = jnp.zeros_like(wide_one)
    for f in range(2):
        for r in range(height):
            wide_one[f, r, 0:width, :] = cache_one[f, r].astype(f32)
    for f in range(2):
        last_line = wide_one[f, jnp.maximum(tall, 1) - 1]
        put_pieces(wide_one[f], last_line, f, tall, wide, sent_one)
    halos_one = halo_copies(counts, lengths_one, sent_one, got_one, send_sems.at[0], recv_sems.at[0])
    for copy in halos_one:
        copy.start()
    for f in range(2):
        last_line = widened(cache_two[f, 2 * jnp.maximum(tall, 1) - 1], fine_breadth)
        frame = widened(cache_two[f], fine_breadth)
        put_pieces(frame, last_line, f, 2 * tall, 2 * wide, sent_two)
    halos_two = halo_copies(counts, lengths_two, sent_two, got_two, send_sems.at[1], recv_sems.at[1])
    for copy in halos_two:
        copy.start()
    if slow > 1:
        hop(1)
    loads[0].wait()
    for copy in halos_one:
        copy.wait()
    for f in range(2):
        extend(wide_one[f], f, tall, wide, got_one, counts, shifted_one)
    if slow > 2:
        hop(2)
    loads[1].wait()
    sum_one[...] = convolve_rows(
        shifted_one, 2, held_one, times, 0, sum_one.shape[0], breadth
    )
    for step in range(3, slow):
        hop(step)
    for copy in halos_two:
        copy.wait()
    for f in range(2):
        frame = widened(cache_two[f], fine_breadth)
        extend(frame, f, 2 * tall, 2 * wide, got_two, counts, shifted_two)
    fine_total = sum_two.shape[0]
    fine_chunk = fine_total // 3 if fine_total % 48 == 0 else fine_total

    def prior_two(part):
        at = part * fine_chunk
        if at < fine_total:
            sum_two[at : at + fine_chunk, :] = convolve_rows(
                shifted_two, 2, held_two, times_t, at, fine_chunk, fine_breadth
            )

    prior_two(0)
    slot = lax.broadcasted_iota(jnp.int32, (1, each), 1)
    slot_row = jnp.zeros((1, each), jnp.int32)
    for r in range(1, height + 1):
        slot_row += jnp.where(slot >= r * width, 1, 0)
    slot_col = slot - slot_row * width
    for c in range(col_count):
        usable = jnp.logical_and(slot_row < tall, slot_col < col_sizes[c])
        bias[c : c + 1, :] = jnp.where(usable, 0.0, masked_score)
    masks = jnp.concatenate([bias[c : c + 1, :] for c in range(col_count)], axis=1)
    lanes = lax.broadcasted_iota(jnp.int32, (each, 128), 1)
    finish()
    for copy in query_copies:
        copy.wait()

    def partial_of(target):
        all_keys = keys[...].reshape(col_count * each, channels)
        scores = times_t(queries[target], all_keys) + masks
        highest = jnp.max(scores, axis=1, keepdims=True)
        expos = jnp.exp2(scores - highest)
        total = jnp.sum(expos, axis=1, keepdims=True)
        mean = times(expos.astype(bf16), all_keys) / total
        level = highest + jnp.log2(total)
        high = level.astype(bf16).astype(f32)
        mid = (level - high).astype(bf16).astype(f32)
        low = level - high - mid
        coded = jnp.where(lanes == 0, high, jnp.where(lanes == 1, mid, jnp.where(lanes == 2, low, 0.0)))
        parts[target, :, 0:channels] = mean.astype(bf16)
        parts[target, :, channels : channels + 128] = coded.astype(bf16)

    copies = []
    for d in sorted(range(1, row_count), key=lambda d: -min(d, row_count - d)):
        target = others[d - 1][0]
        partial_of(target)
        copies.append(
            pltpu.make_async_remote_copy(
                src_ref=parts.at[target],
                dst_ref=got_parts.at[d - 1],
                send_sem=part_send.at[d - 1],
                recv_sem=part_recv.at[d - 1],
                device_id=others[d - 1],
                device_id_type=MESH,
            )
        )
        copies[-1].start()
    partial_of(row)
    prior_two(1)
    for copy in copies:
        copy.wait()
    blocks = [parts[row]] + [got_parts[d] for d in range(row_count - 1)]
    levels = [
        jnp.sum(block[:, channels : channels + 128].astype(f32), axis=1, keepdims=True)
        for block in blocks
    ]
    top = functools.reduce(jnp.maximum, levels)
    weights = [jnp.exp2(level - top) for level in levels]
    total = functools.reduce(jnp.add, weights)
    mean = functools.reduce(
        jnp.add, [w * block[:, 0:channels].astype(f32) for w, block in zip(weights, blocks)]
    )
    mean = (mean / total).astype(bf16)
    attention = times(mean, value_weight[...]).astype(bf16)
    projected = times(attention, out_weight[...])
    mixed = (flat[...] + projected).astype(bf16).astype(f32)
    flat[...] = silu(rms_scale(mixed, gain_one[...][None, :]))
    small[...] = jnp.zeros_like(small)
    for r in range(height):
        small[r, 0:width, :] = flat[r * width : (r + 1) * width, :]
    frame = small[...]
    put_pieces(frame, small[jnp.maximum(tall, 1) - 1], 0, tall, wide, sent_new)
    halos = halo_copies(counts, lengths_one, sent_new, got_new, send_sems.at[2], recv_sems.at[2])
    for copy in halos:
        copy.start()
    prior_two(2)
    for copy in halos:
        copy.wait()
    extend(frame, 0, tall, wide, got_new, counts, shifted_new)
    size_one = height * breadth
    y_one = sum_one[...] + convolve_rows(shifted_new, 1, held_one, times, 0, size_one, breadth, 18)
    y_one = y_one.astype(bf16).astype(f32)
    small[...] = silu(rms_scale(y_one, gain_two[...][None, :])).reshape(height, breadth, channels)
    frame = small[...]
    put_pieces(frame, small[jnp.maximum(tall, 1) - 1], 0, tall, wide, sent_last)
    halos = halo_copies(counts, lengths_one, sent_last, got_last, send_sems.at[3], recv_sems.at[3])
    for copy in halos:
        copy.start()
    channels_out = held_two.shape[1]
    phase_weights[:, channels_out:, :] = jnp.zeros_like(phase_weights[:, channels_out:, :])
    for p in range(2):
        for q in range(2):
            for a in range(2):
                for b in range(2):
                    rows_in = ((0,), (1, 2))[a] if p == 0 else ((0, 1), (2,))[a]
                    cols_in = ((0,), (1, 2))[b] if q == 0 else ((0, 1), (2,))[b]
                    taps = [held_two[18 + 3 * i + j].astype(f32) for i in rows_in for j in cols_in]
                    total = functools.reduce(jnp.add, taps).astype(bf16)
                    phase_weights[p * 8 + q * 4 + a * 2 + b, 0:channels_out, :] = total
    for copy in halos:
        copy.wait()
    extend(frame, 0, tall, wide, got_last, counts, shifted_last)
    for p in range(2):
        for q in range(2):
            phase = jnp.zeros((size_one, phase_weights.shape[1]), f32)
            for a in range(2):
                for b in range(2):
                    first = (p + a) * breadth
                    phase += times_t(
                        shifted_last[0, q + b, first : first + size_one, :],
                        phase_weights[p * 8 + q * 4 + a * 2 + b],
                    )
            for i in range(height):
                for lane in range(fine_sum.shape[0]):
                    fine_sum[lane, 2 * i + p, pl.ds(q, breadth, stride=2), :] = phase[
                        i * breadth : (i + 1) * breadth, lane * 128 : (lane + 1) * 128
                    ]
    fine_height, fine_narrow, channels_out = out.shape
    fine_cols = lax.broadcasted_iota(jnp.int32, (fine_narrow, channels_out), 0)
    for i in range(fine_height):
        keep = jnp.logical_and(fine_cols < 2 * wide, i < 2 * tall)
        for lane in range(fine_sum.shape[0]):
            place = slice(lane * 128, min(lane * 128 + 128, channels_out))
            count = place.stop - place.start
            line = fine_sum[lane, i, 0:fine_narrow, 0:count] + sum_two[i * fine_breadth : i * fine_breadth + fine_narrow, place]
            out[i, :, place] = jnp.where(keep[:, place], line, 0.0).astype(bf16)


def remote_call(kernel, out_shape, kinds, scratch, number, flops):
    return pl.pallas_call(
        kernel,
        out_shape=out_shape,
        in_specs=[pl.BlockSpec(memory_space=kind) for kind in kinds],
        out_specs=jax.tree.map(lambda _: pl.BlockSpec(memory_space=pltpu.VMEM), out_shape),
        scratch_shapes=scratch,
        compiler_params=pltpu.CompilerParams(
            collective_id=number, has_side_effects=True, vmem_limit_bytes=vmem_bytes
        ),
        cost_estimate=pl.CostEstimate(flops=flops, bytes_accessed=20_000_000, transcendentals=0),
    )


def local(
    counts, tokens, row_sizes, col_sizes, norm_gain, query_weight, key_weight, value_weight,
    out_weight, cache_one, gain_one, conv_one, cache_two, gain_two, conv_two,
):
    height, width, channels = tokens.shape
    channels_out = conv_two.shape[-1]
    rows, cols = counts
    breadth = round_up(width + 1, 16)
    fine_breadth = round_up(2 * width + 1, 16)
    each = round_up(height * width, 16)

    kernels_one = conv_one.reshape(27, channels, channels)
    kernels_two = jnp.swapaxes(conv_two, 3, 4).reshape(27, channels_out, channels)
    line_one = max(breadth, round_up(height, 16))
    line_two = max(fine_breadth, round_up(2 * height, 16))
    lanes_out = round_up(channels_out, 128)
    fast = fast_part(cols)
    slow = cols // fast
    vm, sm, dma = pltpu.VMEM, pltpu.SMEM, pltpu.SemaphoreType.DMA
    shape = jax.ShapeDtypeStruct
    return remote_call(
        functools.partial(whole_kernel, counts),
        shape((2 * height, 2 * width, channels_out), bf16),
        [sm] * 2 + [vm] * 10 + [pl.ANY] * 2,
        [
            vm((height * breadth, channels), f32),
            vm((2 * height * fine_breadth, channels_out), f32),
            vm((cols, each, channels), bf16),
            vm((rows, each, channels), bf16),
            vm((16, lanes_out, channels), bf16),
            vm((rows, each, channels + 128), bf16),
            vm((rows - 1, each, channels + 128), bf16),
            vm((round_up(cols, 8), each), f32),
            vm((each, channels), f32),
            vm((height, breadth, channels), f32),
            vm((2, height, breadth, channels), f32),
            vm((lanes_out // 128, 2 * height, 2 * breadth, 128), f32),
            vm((8, 2, line_one, channels), bf16),
            vm((8, 2, line_one, channels), bf16),
            vm((8, 2, line_two, channels), bf16),
            vm((8, 2, line_two, channels), bf16),
            vm((8, 1, line_one, channels), bf16),
            vm((8, 1, line_one, channels), bf16),
            vm((8, 1, line_one, channels), bf16),
            vm((8, 1, line_one, channels), bf16),
            vm((2, 3, (height + 2) * breadth, channels), bf16),
            vm((2, 3, (2 * height + 2) * fine_breadth, channels), bf16),
            vm((1, 3, (height + 2) * breadth, channels), bf16),
            vm((1, 3, (height + 2) * breadth, channels), bf16),
            vm((27, channels, channels), bf16),
            vm((27, channels_out, channels), bf16),
            dma((4, 8)),
            dma((4, 8)),
            dma((rows - 1,)),
            dma((rows - 1,)),
            dma((slow,)),
            dma((slow,)),
            dma((max(fast - 1, 1), slow)),
            dma((cols,)),
            dma((2,)),
            dma((rows - 1,)),
            dma((rows - 1,)),
        ],
        1,
        18_000_000_000,
    )(
        row_sizes, col_sizes, tokens, norm_gain, query_weight, key_weight, value_weight, out_weight,
        cache_one, gain_one, cache_two, gain_two, kernels_one, kernels_two,
    )


def solution(mesh):
    tiled = P("row", "col", None)
    framed = P(None, "row", "col", None)
    placed = (tiled,) + (P(),) * 7 + (framed, P(), P(), framed, P(), P())
    counts = (mesh.shape["row"], mesh.shape["col"])
    return jax.shard_map(
        functools.partial(local, counts),
        mesh=mesh,
        in_specs=placed,
        out_specs=P("row", "col", None),
        check_vma=False,
    )
```
